128 devices in a mesh: rep: 16 (over y_hi, z, core), tp: 8 (over x, y_lo).
Axes of the slice: x: 4, y: 4 (y_hi: 2, y_lo: 2; y = y_hi * 2 + y_lo), z: 4, core: 2. Of those that a mesh axis runs over, the one named last changes fastest.
Arguments:
- hidden_in: bfloat16 [4, 2048, 5120], P(None, 'rep'), may hold values from -6 to 6
- ln_gain: float32 [5120], replicated, may hold values from 0.1 to 1.9
- q_gain: float32 [128], replicated, may hold values from 0.1 to 1.9
- k_gain: float32 [128], replicated, may hold values from 0.1 to 1.9
- w_query: bfloat16 [5120, 8192], P(('rep', 'tp')), may hold values from -0.09782797 to 0.09782797
- w_key: bfloat16 [5120, 1024], P(('rep', 'tp')), may hold values from -0.09782797 to 0.09782797
- w_value: bfloat16 [5120, 1024], P(('rep', 'tp')), may hold values from -0.09782797 to 0.09782797
- w_out: bfloat16 [8192, 5120], P('tp', 'rep'), may hold values from -0.077339804 to 0.077339804
- cache_keys: bfloat16 [2048, 64, 1024], P('rep', None, 'tp'), may hold values from -300 to 300
- cache_values: bfloat16 [2048, 64, 1024], P('rep', None, 'tp'), may hold values from -6 to 6
- cache_lengths: int32 [2048], P('rep'), may hold values from 1 to 64, as said below
- amax_history: float32 [4, 16], replicated, may hold values from 0.7 to 2.8
- cycle_pos: int32 [4], replicated, may hold values from 0 to 15
Outputs:
- mixed_out: bfloat16 [4, 2048, 5120], P(None, 'rep', 'tp')
- new_history: float32 [4, 16], replicated
The draws below stay inside these ranges and needn't reach their ends.
Inputs may be any that keep to these rules, and one draw needn't show every extreme that they name: `cache_lengths`: among the 128 sequences of each replica at least one holds exactly 64 cached tokens.
All inputs are finite; a program needn't handle non-finite values.
Results may differ from the reference program's by a relative error of at most 0.0086.
Values may be sent and summed in bfloat16 or wider, within the bound.
A program may use at most 192 MiB of HBM per device.

```python
import math
import jax
import jax.numpy as jnp
from jax import lax

D = 5120
HEADS = 64
KV_HEADS = 8
HEAD_DIM = 128
ROWS_REP = 128
CACHE = 64
STEPS = 4
HIST = 16
WINDOW = 8
Q_WIDTH = 8192
KV_WIDTH = 1024
ROWS = 2048


def rising(key, row_count, col_count, fan_in, row_part, col_part):
    base = jax.random.truncated_normal(key, -4.0, 4.0, (row_count, col_count), jnp.float32)
    down_rows = jnp.arange(row_count, dtype=jnp.float32)[:, None] / (row_count - 1)
    across = jnp.arange(col_count, dtype=jnp.float32)[None, :] / (col_count - 1)
    growth = jnp.exp(math.log(3.0) * (row_part * down_rows + col_part * across))
    return (base * growth / (1.8 * math.sqrt(fan_in))).astype(jnp.bfloat16)


def draw_w_query(key, part):
    key = jax.random.fold_in(key, 3)
    return rising(key, D, Q_WIDTH, D, 1.0, 0.0)


def draw_w_key(key, part):
    key = jax.random.fold_in(key, 5)
    return rising(key, D, KV_WIDTH, D, 1.0, 0.0)


def draw_w_value(key, part):
    key = jax.random.fold_in(key, 7)
    return rising(key, D, KV_WIDTH, D, 1.0, 0.0)


def draw_w_out(key, part):
    key = jax.random.fold_in(key, 9)
    return rising(key, Q_WIDTH, D, Q_WIDTH, 0.5, 0.5)


def draw_cache_keys(key, part):
    key = jax.random.fold_in(key, 11)
    base = jax.random.truncated_normal(key, -6.0, 6.0, (ROWS, CACHE, KV_WIDTH), jnp.float32)
    return base.astype(jnp.bfloat16)


def draw_cache_lengths(key, part):
    key = jax.random.fold_in(key, 13)
    first_key, second_key = jax.random.split(key)
    drawn = jax.random.randint(first_key, (ROWS,), 1, CACHE + 1)
    chosen = jax.random.randint(second_key, (ROWS // ROWS_REP,), 0, ROWS_REP)
    row_index = jnp.arange(ROWS)
    filled = row_index % ROWS_REP == chosen[row_index // ROWS_REP]
    return jnp.where(filled, CACHE, drawn).astype(jnp.int32)


def place_ends(entries, own_key, low, high):
    dims = entries.shape
    spot = [jax.random.randint(jax.random.fold_in(own_key, axis), (), 0, dims[axis]) for axis in range(len(dims))]
    entries = entries.at[tuple(spot)].set(low)
    longest = dims.index(max(dims))
    spot[longest] = (spot[longest] + 1) % dims[longest]
    return entries.at[tuple(spot)].set(high)


def level_of(stream_key, dims, cuts, smallest, high):
    factor_of = 1.0
    for axis_at, blocks in cuts:
        heights = jax.random.uniform(jax.random.fold_in(jax.random.fold_in(stream_key, 6), axis_at), (blocks,), jnp.float32, smallest / len(cuts), high / len(cuts))
        factor_of = factor_of * jnp.repeat(jnp.exp(heights), dims[axis_at] // blocks).reshape((-1,) + (1,) * (len(dims) - 1 - axis_at))
    return factor_of


def normal_values(key, extent, scale, limit, shards=(), kind=jnp.bfloat16):
    values = scale * jax.random.normal(key, extent, jnp.float32)
    if shards:
        values = values * level_of(key, extent, shards, -0.22, 0.18)
    return jnp.clip(values, -limit, limit).astype(kind)


def setup_inputs(seed: int = 0) -> dict:
    seeds = jax.random.split(jax.random.key(seed), 14)
    hidden_in = normal_values(seeds[0], (STEPS, ROWS, D), 1.0, 6.0, ((1, 16),))
    ln_gain = jnp.clip(1.0 + 0.18 * jax.random.normal(seeds[1], (D,), jnp.float32), 0.1, 1.9)
    q_gain = jnp.clip(1.0 + 0.18 * jax.random.normal(seeds[2], (HEAD_DIM,), jnp.float32), 0.1, 1.9)
    k_gain = jnp.clip(1.0 + 0.18 * jax.random.normal(seeds[3], (HEAD_DIM,), jnp.float32), 0.1, 1.9)
    w_query = draw_w_query(jax.random.fold_in(seeds[13], 71), 0)
    w_key = draw_w_key(jax.random.fold_in(seeds[13], 71), 0)
    w_value = draw_w_value(jax.random.fold_in(seeds[13], 71), 0)
    w_out = draw_w_out(jax.random.fold_in(seeds[13], 71), 0)
    cache_keys = draw_cache_keys(jax.random.fold_in(seeds[13], 71), 0)
    cache_values = normal_values(seeds[9], (ROWS, CACHE, KV_WIDTH), 1.0, 6.0, ((0, 16), (2, 8)))
    cache_lengths = draw_cache_lengths(jax.random.fold_in(seeds[13], 71), 0)
    amax_history = jnp.clip(jnp.exp(jax.random.uniform(seeds[11], (4, HIST), jnp.float32, math.log(0.7), math.log(2.8))), 0.7, 2.8)
    cycle_pos = place_ends(jax.random.randint(seeds[12], (4,), 0, HIST), jax.random.fold_in(seeds[12], 1), 0, HIST - 1).astype(jnp.int32)
    return {"hidden_in": hidden_in, "ln_gain": ln_gain, "q_gain": q_gain, "k_gain": k_gain, "w_query": w_query, "w_key": w_key, "w_value": w_value, "w_out": w_out, "cache_keys": cache_keys, "cache_values": cache_values, "cache_lengths": cache_lengths, "amax_history": amax_history, "cycle_pos": cycle_pos}


fp8_top = 448.0
rope_base = 1000000.0
norm_eps = 1e-06

def fan_roots():
    return jnp.sqrt(jnp.array([D, D, D, Q_WIDTH], dtype=jnp.float32))

def window_amax(history, cycle_pos):
    slot_index = jnp.arange(HIST, dtype=jnp.int32)
    behind = (cycle_pos[:, None] - 1 - slot_index[None, :]) % HIST
    return lax.optimization_barrier(jnp.max(jnp.where(behind < WINDOW, history, 0.0), axis=1))

def quantize(weight, factor):
    return jnp.clip(weight.astype(jnp.float32) / factor, -fp8_top, fp8_top).astype(jnp.bfloat16)

def rms_scale(values, gain):
    mean_square = lax.optimization_barrier(jnp.mean(values * values, axis=-1, keepdims=True))
    return values * lax.rsqrt(mean_square + norm_eps) * gain

def rotate(values, positions):
    half_dim = HEAD_DIM // 2
    inverse = rope_base ** (-(2.0 * jnp.arange(half_dim, dtype=jnp.float32)) / HEAD_DIM)
    angles = positions.astype(jnp.float32)[:, None, None] * inverse
    cosine = jnp.cos(angles)
    sine_part = jnp.sin(angles)
    leading = values[..., :half_dim]
    trailing = values[..., half_dim:]
    return jnp.concatenate([leading * cosine - trailing * sine_part, trailing * cosine + leading * sine_part], axis=-1)

def attend(queries, new_keys, new_values, cache_keys, cache_values, cache_lengths):
    row_count = cache_keys.shape[0]
    slot_count = cache_keys.shape[1]
    kv_local = new_keys.shape[1] // HEAD_DIM
    group_size = HEADS // KV_HEADS
    group_queries = queries.reshape(STEPS, row_count, kv_local, group_size, HEAD_DIM).transpose(1, 2, 0, 3, 4)
    group_queries = group_queries.reshape(row_count, kv_local, STEPS * group_size, HEAD_DIM).astype(jnp.float32)
    fresh_keys = new_keys.reshape(STEPS, row_count, kv_local, HEAD_DIM).astype(jnp.float32)
    fresh_values = new_values.reshape(STEPS, row_count, kv_local, HEAD_DIM).astype(jnp.float32)
    old_keys = cache_keys.reshape(row_count, slot_count, kv_local, HEAD_DIM).astype(jnp.float32)
    old_values = cache_values.reshape(row_count, slot_count, kv_local, HEAD_DIM).astype(jnp.float32)
    scaling = HEAD_DIM ** (-0.5)
    score_old = jnp.einsum('rkqd,rckd->rkqc', group_queries, old_keys) * scaling
    score_new = jnp.einsum('rkqd,urkd->rkqu', group_queries, fresh_keys) * scaling
    live_old = jnp.arange(slot_count, dtype=jnp.int32)[None, :] < cache_lengths[:, None]
    step_of = jnp.arange(STEPS * group_size, dtype=jnp.int32) // group_size
    live_new = jnp.arange(STEPS, dtype=jnp.int32)[None, :] <= step_of[:, None]
    score_old = jnp.where(live_old[:, None, None, :], score_old, -jnp.inf)
    score_new = jnp.where(live_new[None, None, :, :], score_new, -jnp.inf)
    row_top = jnp.maximum(lax.optimization_barrier(jnp.max(score_old, axis=-1)), lax.optimization_barrier(jnp.max(score_new, axis=-1)))
    raised_old = jnp.exp(score_old - row_top[..., None])
    raised_new = jnp.exp(score_new - row_top[..., None])
    denominator = lax.optimization_barrier(jnp.sum(raised_old, axis=-1)) + lax.optimization_barrier(jnp.sum(raised_new, axis=-1))
    share_old = (raised_old / denominator[..., None]).astype(jnp.bfloat16).astype(jnp.float32)
    share_new = (raised_new / denominator[..., None]).astype(jnp.bfloat16).astype(jnp.float32)
    result = jnp.einsum('rkqc,rckd->rkqd', share_old, old_values) + jnp.einsum('rkqu,urkd->rkqd', share_new, fresh_values)
    result = result.astype(jnp.bfloat16).reshape(row_count, kv_local, STEPS, group_size, HEAD_DIM)
    return result.transpose(2, 0, 1, 3, 4).reshape(STEPS * row_count, kv_local * group_size * HEAD_DIM)

def reference(hidden_in, ln_gain, q_gain, k_gain, w_query, w_key, w_value, w_out, cache_keys, cache_values, cache_lengths, amax_history, cycle_pos):
    roots = fan_roots()
    scales = window_amax(amax_history, cycle_pos) / (fp8_top * roots)
    current = jnp.stack([jnp.max(jnp.abs(w_query)).astype(jnp.float32), jnp.max(jnp.abs(w_key)).astype(jnp.float32), jnp.max(jnp.abs(w_value)).astype(jnp.float32), jnp.max(jnp.abs(w_out)).astype(jnp.float32)]) * roots
    slot_index = jnp.arange(HIST, dtype=jnp.int32)
    new_history = jnp.where(slot_index[None, :] == cycle_pos[:, None], current[:, None], amax_history)
    total_rows = STEPS * ROWS
    flat_rows = hidden_in.reshape(total_rows, D)
    normed = rms_scale(flat_rows.astype(jnp.float32), ln_gain).astype(jnp.bfloat16)
    queries = jnp.dot(normed, quantize(w_query, scales[0]), preferred_element_type=jnp.float32)
    new_keys = jnp.dot(normed, quantize(w_key, scales[1]), preferred_element_type=jnp.float32)
    new_values = jnp.dot(normed, quantize(w_value, scales[2]), preferred_element_type=jnp.float32)
    positions = (cache_lengths[None, :] + jnp.arange(STEPS, dtype=jnp.int32)[:, None]).reshape(total_rows)
    queries = rotate(rms_scale(queries.reshape(total_rows, HEADS, HEAD_DIM), q_gain), positions)
    queries = queries.astype(jnp.bfloat16).reshape(total_rows, Q_WIDTH)
    new_keys = rotate(rms_scale(new_keys.reshape(total_rows, KV_HEADS, HEAD_DIM), k_gain), positions)
    new_keys = new_keys.astype(jnp.bfloat16).reshape(total_rows, KV_WIDTH)
    new_values = (new_values * scales[2]).astype(jnp.bfloat16)
    attended = attend(queries, new_keys, new_values, cache_keys, cache_values, cache_lengths)
    branch = jnp.dot(attended, quantize(w_out, scales[3]), preferred_element_type=jnp.float32) * scales[3]
    mixed_out = (flat_rows.astype(jnp.float32) + branch).astype(jnp.bfloat16).reshape(STEPS, ROWS, D)
    return (mixed_out, new_history)
```

```python
import jax
import jax.numpy as jnp
import numpy as np
from jax import lax
from jax.experimental import pallas as pl
from jax.experimental.pallas import tpu as pltpu
from jax.sharding import PartitionSpec as P

D = 5120
HEADS = 64
KV_HEADS = 8
HEAD_DIM = 128
STEPS = 4
HIST = 16
WINDOW = 8
Q_WIDTH = 8192
CACHE = 64
SEQS = 128
ROWS = STEPS * SEQS
REPS = 16
TPS = 8
SPOTS = 8
SHARD = 40
Q_LOCAL = 1024
HALF = 640
PACKED = 80
OUT_SHARD = 320

fp8_top = 448.0
rope_base = 1000000.0
norm_eps = 1e-06

BF = jnp.bfloat16
F32 = jnp.float32
MESH = pl.DeviceIdType.MESH


def spread_matrices():
    place = np.zeros((2, HALF, 768), np.float32)
    for block in range(16):
        for row in range(32):
            place[0, block * SHARD + row, block * 48 + row] = 1.0
            place[1, block * SHARD + row, block * 48 + 16 + row] = 1.0
        for row in range(8):
            place[0, block * SHARD + 32 + row, block * 48 + 32 + row] = 1.0
            place[1, block * SHARD + 32 + row, block * 48 + 8 + row] = 1.0
    return place


def join_matrices():
    place = np.zeros((2, 384, HALF), np.float32)
    for col in range(OUT_SHARD):
        place[0, col, col] = 1.0
        place[1, col, OUT_SHARD + col] = 1.0
    return place


def dot(a, b):
    return jnp.dot(a, b, preferred_element_type=F32)


def quantize(weight, factor):
    return jnp.clip(weight.astype(F32) / factor, -fp8_top, fp8_top)


def kernel(
    hidden,
    ln_gain,
    q_gain,
    k_gain,
    w_query,
    w_key,
    w_value,
    w_out,
    cache_keys,
    cache_values,
    lengths,
    history,
    cycle,
    spread,
    join,
    freq,
    mixed,
    new_history,
    rows_in,
    keys_in,
    values_in,
    stage,
    wbuf,
    obuf,
    oshard,
    oside,
    xp,
    acc,
    att,
    attb,
    rs_send,
    rs_recv,
    resid,
    amax_out,
    amax_in,
    local_sem,
    a2a_s,
    a2a_r,
    w_s,
    w_r,
    o_s,
    o_r,
    side_s,
    side_r,
    rs_s,
    rs_r,
    am_s,
    am_r,
):
    rep = lax.axis_index("rep")
    tp = lax.axis_index("tp")
    yh = rep // 8
    zz = (rep // 2) % 4
    core = rep % 2
    spot = rep // 2

    def rep_of(dy, dz, flip):
        return ((yh + dy) % 2) * 8 + ((zz + dz) % 4) * 2 + (core + flip) % 2

    def spot_of(dy, dz):
        return ((yh + dy) % 2) * 4 + (zz + dz) % 4

    def at_rep(index):
        return {"rep": index, "tp": tp}

    def at_tp(index):
        return {"rep": rep, "tp": index}

    peers = [(tp + s) % TPS for s in range(1, TPS)]
    y_far = rep_of(1, 0, 0)
    z_up = rep_of(0, 1, 0)
    z_down = rep_of(0, 3, 0)
    sibling = rep_of(0, 0, 1)

    loads = []
    for i in range(SPOTS):
        loads.append(
            pltpu.make_async_copy(hidden.at[:, pl.ds(i * HALF, HALF)], rows_in.at[i], local_sem.at[i])
        )
    loads.append(pltpu.make_async_copy(cache_keys, keys_in, local_sem.at[8]))
    loads.append(pltpu.make_async_copy(cache_values, values_in, local_sem.at[9]))
    loads.append(
        pltpu.make_async_copy(
            hidden.at[:, pl.ds(pl.multiple_of(tp * HALF, 128), HALF)], resid, local_sem.at[10]
        )
    )
    for load in loads:
        load.start()

    barrier = pltpu.get_barrier_semaphore()
    for peer in peers:
        pl.semaphore_signal(barrier, inc=1, device_id=at_tp(peer), device_id_type=MESH)
    for other in (y_far, z_up, z_down, sibling):
        pl.semaphore_signal(barrier, inc=1, device_id=at_rep(other), device_id_type=MESH)

    slot = lax.broadcasted_iota(jnp.int32, (1, HIST), 1)
    fans = (D, D, D, Q_WIDTH)
    roots = [float(np.sqrt(np.float32(fan))) for fan in fans]
    scales = []
    for m in range(4):
        behind = jnp.bitwise_and(cycle[m] + (2 * HIST - 1) - slot, HIST - 1)
        limit = jnp.max(
            jnp.where(behind < WINDOW, history[m : m + 1, :], 0.0), axis=1, keepdims=True
        )
        scales.append(limit / (fp8_top * roots[m]))

    def pack(j, tops):
        query = w_query[:, pl.ds(pl.multiple_of(j * Q_LOCAL, 128), Q_LOCAL)]
        key = w_key[:, pl.ds(pl.multiple_of(j * 128, 128), 128)]
        value = w_value[:, pl.ds(pl.multiple_of(j * 128, 128), 128)]
        q0 = quantize(query, scales[0])
        k0 = quantize(key, scales[1])
        v0 = quantize(value, scales[2])
        first = q0[:, :HALF]
        second = jnp.concatenate([q0[:, HALF:], k0, v0], axis=1)
        stage[j, 0:32, :] = first[0:32].astype(BF)
        stage[j, 32:48, :] = jnp.concatenate([first[32:40], second[32:40]], axis=0).astype(BF)
        stage[j, 48:80, :] = second[0:32].astype(BF)

        def top(values, old):
            found = jnp.max(jnp.abs(values.astype(F32)), axis=0, keepdims=True)
            for i in range(values.shape[1] // 128):
                old = jnp.maximum(old, found[:, i * 128 : (i + 1) * 128])
            return old

        return top(query, tops[0]), top(key, tops[1]), top(value, tops[2])

    none = jnp.zeros((1, 128), F32)
    tops = lax.fori_loop(0, TPS, pack, (none, none, none))

    pl.semaphore_wait(barrier, 11)

    a2a = []
    for s, peer in enumerate(peers):
        a2a.append(
            pltpu.make_async_remote_copy(
                src_ref=stage.at[peer],
                dst_ref=wbuf.at[rep, tp],
                send_sem=a2a_s.at[s],
                recv_sem=a2a_r.at[s],
                device_id=at_tp(peer),
                device_id_type=MESH,
            )
        )
    for copy in a2a:
        copy.start()
    own_plane = pltpu.make_async_copy(stage.at[tp], wbuf.at[rep, tp], local_sem.at[11])
    own_plane.start()

    def pack_out(i, old):
        rows = pl.ds(pl.multiple_of(i * 128, 128), 128)
        shard = w_out[rows, :]
        ready = quantize(shard, scales[3])
        oshard[rows, :] = jnp.concatenate([ready, jnp.zeros((128, 64), F32)], axis=1).astype(BF)
        found = jnp.max(jnp.abs(shard.astype(F32)), axis=0, keepdims=True)
        return jnp.maximum(old, jnp.max(found, axis=1, keepdims=True))

    top_out = lax.fori_loop(0, 8, pack_out, jnp.zeros((1, 1), F32))
    side = pltpu.make_async_remote_copy(
        src_ref=oshard.at[pl.ds(pl.multiple_of((1 - core) * 512, 512), 512)],
        dst_ref=oside,
        send_sem=side_s,
        recv_sem=side_r,
        device_id=at_rep(sibling),
        device_id_type=MESH,
    )
    side.start()

    tile_row = lax.broadcasted_iota(jnp.int32, (8, 128), 0)
    found = [jnp.max(top, axis=1, keepdims=True) for top in tops] + [top_out]
    tile = jnp.zeros((8, 128), F32)
    for m in range(4):
        tile = jnp.where(tile_row == m, found[m], tile)
    amax_out[0] = tile

    def send_amax(stage_index, slot_index, where):
        return pltpu.make_async_remote_copy(
            src_ref=amax_out.at[stage_index],
            dst_ref=amax_in.at[slot_index],
            send_sem=am_s.at[slot_index],
            recv_sem=am_r.at[slot_index],
            device_id=where,
            device_id_type=MESH,
        )

    am_tp = [send_amax(0, s, at_tp(peer)) for s, peer in enumerate(peers)]
    am_y = [send_amax(1, 7, at_rep(y_far))]
    am_z = [send_amax(2, 8, at_rep(z_up)), send_amax(2, 9, at_rep(z_down))]
    am_w = [send_amax(3, 10, at_rep(z_up))]
    am_c = [send_amax(4, 11, at_rep(sibling))]

    def fold(copies, index, slots):
        for copy in copies:
            copy.wait()
        total = amax_out[index]
        for where in slots:
            total = jnp.maximum(total, amax_in[where])
        amax_out[index + 1] = total

    for copy in am_tp:
        copy.start()

    for load in loads[:8]:
        load.wait()

    def norm(i, carry):
        rows = pl.ds(pl.multiple_of(i * 32, 32), 32)
        parts = [rows_in[j, rows, :].astype(F32) for j in range(SPOTS)]
        square = parts[0] * parts[0]
        for part in parts[1:]:
            square = square + part * part
        mean = jnp.sum(square, axis=1, keepdims=True) / D
        factor = lax.rsqrt(mean + norm_eps)
        for j in range(SPOTS):
            gain = ln_gain[0:1, j * HALF : (j + 1) * HALF]
            rows_in[j, rows, :] = (parts[j] * factor * gain).astype(BF)
        return carry

    lax.fori_loop(0, ROWS // 32, norm, 0)

    def relay(buf, view, send_sem, recv_sem):
        sent = []

        def send(block, half, target):
            copy = pltpu.make_async_remote_copy(
                src_ref=view(buf, block, half),
                dst_ref=view(buf, block, half),
                send_sem=send_sem.at[len(sent)],
                recv_sem=recv_sem.at[block, half],
                device_id=at_rep(target),
                device_id_type=MESH,
            )
            copy.start()
            sent.append(copy)

        def arrive(block, half):
            pltpu.make_async_remote_copy(
                src_ref=view(buf, block, half),
                dst_ref=view(buf, block, half),
                send_sem=send_sem.at[0],
                recv_sem=recv_sem.at[block, half],
                device_id=at_rep(sibling),
                device_id_type=MESH,
            ).wait_recv()

        return send, arrive, sent

    def view_w(buf, block, half):
        return buf.at[block, pl.ds(half * 4, 4)]

    def view_o(buf, block, half):
        return buf.at[block, pl.ds(half * 256, 256)]

    send_w, arrive_w, sent_w = relay(wbuf, view_w, w_s, w_r)
    send_o, arrive_o, sent_o = relay(obuf, view_o, o_s, o_r)

    def own(send):
        for half in range(2):
            for target in (y_far, z_up, z_down, sibling):
                send(rep, half, target)

    def far(send, arrive):
        for half in range(2):
            arrive(y_far, half)
            for target in (z_up, z_down, sibling):
                send(y_far, half, target)

    def beside(send, arrive, dy, dz):
        block = rep_of(dy, dz, 0)
        target, keep = (z_down, 0) if dz == 1 else (z_up, 1)
        for half in range(2):
            arrive(block, half)
            if half == keep:
                send(block, half, target)
            send(block, half, sibling)

    def across(send, arrive, dy):
        block = rep_of(dy, 2, 0)
        for half in range(2):
            arrive(block, half)
            send(block, half, sibling)

    def from_sibling(arrive, dy, dz):
        block = rep_of(dy, dz, 1)
        for half in range(2):
            arrive(block, half)

    side.wait()
    mine = pl.ds(pl.multiple_of(core * 512, 512), 512)
    obuf[rep] = (dot(oshard[mine, :], join[core]) + dot(oside[...], join[1 - core])).astype(BF)
    own(send_o)

    own_plane.wait()
    for copy in a2a:
        copy.wait()
    own(send_w)

    acc[...] = jnp.zeros_like(acc)

    def project(dy, dz):
        place = spot_of(dy, dz)
        for h in range(2):
            def tiles(i, carry):
                rows = pl.ds(pl.multiple_of(i * 256, 256), 256)
                xs = dot(rows_in[place, rows, :], spread[h]).astype(BF)
                total = acc[h, rows, :]
                for cc in range(2):
                    block = wbuf[place * 2 + cc, :, h * 32 : h * 32 + 48, :].reshape(384, HALF)
                    total = total + dot(xs[:, cc * 384 : (cc + 1) * 384], block)
                acc[h, rows, :] = total
                return carry

            lax.fori_loop(0, 2, tiles, 0)

    from_sibling(arrive_w, 0, 0)
    project(0, 0)
    fold(am_tp, 0, range(7))
    am_y[0].start()
    far(send_w, arrive_w)
    beside(send_w, arrive_w, 0, 1)
    beside(send_w, arrive_w, 0, 3)
    from_sibling(arrive_w, 1, 0)
    project(1, 0)
    fold(am_y, 1, [7])
    for copy in am_z:
        copy.start()
    from_sibling(arrive_w, 0, 1)
    project(0, 1)
    from_sibling(arrive_w, 0, 3)
    project(0, 3)
    fold(am_z, 2, [8, 9])
    am_w[0].start()
    beside(send_w, arrive_w, 1, 1)
    beside(send_w, arrive_w, 1, 3)
    far(send_o, arrive_o)
    beside(send_o, arrive_o, 0, 1)
    beside(send_o, arrive_o, 0, 3)
    from_sibling(arrive_w, 1, 1)
    project(1, 1)
    from_sibling(arrive_w, 1, 3)
    project(1, 3)
    fold(am_w, 3, [10])
    am_c[0].start()
    across(send_w, arrive_w, 0)
    from_sibling(arrive_w, 0, 2)
    project(0, 2)
    across(send_w, arrive_w, 1)
    from_sibling(arrive_w, 1, 2)
    project(1, 2)
    fold(am_c, 4, [11])
    history_row = lax.broadcasted_iota(jnp.int32, (1, HIST), 1)
    for m in range(4):
        new_history[m : m + 1, :] = jnp.where(
            history_row == cycle[m],
            amax_out[5, m : m + 1, 0:1] * roots[m],
            history[m : m + 1, :],
        )

    def head_norm(s, carry):
        rows = pl.ds(pl.multiple_of(s * SEQS, SEQS), SEQS)
        angles = (lengths[...] + s).astype(F32) * freq[...]
        cosine = jnp.cos(angles)
        sine = jnp.sin(angles)
        lane = lax.broadcasted_iota(jnp.int32, (SEQS, HEAD_DIM), 1)
        sine = jnp.where(lane < 64, -sine, sine)
        for head in range(9):
            h, lanes = (0, head) if head < 5 else (1, head - 5)
            cols = pl.ds(lanes * HEAD_DIM, HEAD_DIM)
            values = acc[h, rows, cols]
            gain = q_gain[...] if head < 8 else k_gain[...]
            mean = jnp.sum(values * values, axis=1, keepdims=True) / HEAD_DIM
            values = values * lax.rsqrt(mean + norm_eps) * gain
            acc[h, rows, cols] = values * cosine + pltpu.roll(values, 64, 1) * sine
        cols = pl.ds(512, HEAD_DIM)
        acc[1, rows, cols] = acc[1, rows, cols] * scales[2]
        return carry

    lax.fori_loop(0, STEPS, head_norm, 0)

    for load in loads[8:]:
        load.wait()

    old_seq = lax.broadcasted_iota(jnp.int32, (8, 8 * CACHE), 0)
    old_col = lax.broadcasted_iota(jnp.int32, (8, 8 * CACHE), 1)
    old_slot = jnp.where(
        jnp.right_shift(old_col, 6) == old_seq, jnp.bitwise_and(old_col, CACHE - 1), CACHE
    )
    new_row = lax.broadcasted_iota(jnp.int32, (32, 32), 0)
    new_col = lax.broadcasted_iota(jnp.int32, (32, 32), 1)
    new_live = (jnp.bitwise_and(new_row, 7) == jnp.bitwise_and(new_col, 7)) & (
        jnp.right_shift(new_col, 3) <= jnp.right_shift(new_row, 3)
    )
    new_bias = jnp.where(new_live, 0.0, -1e30)
    scaling = HEAD_DIM ** (-0.5)
    nt = (((1,), (1,)), ((), ()))

    def attend(g, carry):
        first = pl.multiple_of(g * 8, 8)
        seqs = pl.ds(first, 8)

        def pick(h, lanes):
            return [
                acc[h, pl.ds(pl.multiple_of(s * SEQS + g * 8, 8), 8), pl.ds(lanes * HEAD_DIM, HEAD_DIM)]
                for s in range(STEPS)
            ]

        rows = []
        for head in range(8):
            rows += pick(0, head) if head < 5 else pick(1, head - 5)
        queries = jnp.concatenate(rows, axis=0).astype(BF)
        fresh_keys = jnp.concatenate(pick(1, 3), axis=0).astype(BF)
        fresh_values = jnp.concatenate(pick(1, 4), axis=0).astype(BF)
        old_keys = keys_in[seqs].reshape(8 * CACHE, HEAD_DIM)
        old_values = values_in[seqs].reshape(8 * CACHE, HEAD_DIM)
        old_bias = jnp.where(old_slot < lengths[seqs, :], 0.0, -1e30)
        old = lax.dot_general(queries, old_keys, nt, preferred_element_type=F32)
        new = lax.dot_general(queries, fresh_keys, nt, preferred_element_type=F32)
        old = (old.reshape(32, 8, 8 * CACHE) * scaling + old_bias[None]).reshape(256, 8 * CACHE)
        new = (new.reshape(8, 32, 32) * scaling + new_bias[None]).reshape(256, 32)
        top = jnp.maximum(
            jnp.max(old, axis=1, keepdims=True), jnp.max(new, axis=1, keepdims=True)
        )
        old = jnp.exp(old - top)
        new = jnp.exp(new - top)
        total = jnp.sum(old, axis=1, keepdims=True) + jnp.sum(new, axis=1, keepdims=True)
        result = dot(old.astype(BF), old_values) + dot(new.astype(BF), fresh_values)
        result = result / total
        for head in range(8):
            for s in range(STEPS):
                start = head * 32 + s * 8
                att[
                    pl.ds(pl.multiple_of(s * SEQS + g * 8, 8), 8),
                    pl.ds(head * HEAD_DIM, HEAD_DIM),
                ] = result[start : start + 8]
        return carry

    lax.fori_loop(0, SEQS // 8, attend, 0)

    def settle(i, carry):
        rows = pl.ds(pl.multiple_of(i * 64, 64), 64)
        attb[rows, :] = att[rows, :].astype(BF)
        return carry

    lax.fori_loop(0, ROWS // 64, settle, 0)

    beside(send_o, arrive_o, 1, 1)
    beside(send_o, arrive_o, 1, 3)
    across(send_o, arrive_o, 0)
    across(send_o, arrive_o, 1)
    for dy in range(2):
        for dz in range(4):
            from_sibling(arrive_o, dy, dz)

    def partial(owner, rows):
        weights = obuf[pl.ds(owner * 2, 2)].reshape(Q_LOCAL, HALF)
        return dot(attb[rows, :], weights)

    sums = []
    for s, peer in enumerate(peers):
        def tiles(i, carry):
            rows = pl.ds(pl.multiple_of(i * 256, 256), 256)
            rs_send[s, rows, :] = partial(peer, rows).astype(BF)
            return carry

        lax.fori_loop(0, 2, tiles, 0)
        copy = pltpu.make_async_remote_copy(
            src_ref=rs_send.at[s],
            dst_ref=rs_recv.at[s],
            send_sem=rs_s.at[s],
            recv_sem=rs_r.at[s],
            device_id=at_tp(peer),
            device_id_type=MESH,
        )
        copy.start()
        sums.append(copy)

    def tiles_own(i, carry):
        rows = pl.ds(pl.multiple_of(i * 256, 256), 256)
        acc[0, rows, :] = partial(tp, rows)
        return carry

    lax.fori_loop(0, 2, tiles_own, 0)
    for copy in sums:
        copy.wait_recv()

    def finish(i, carry):
        rows = pl.ds(pl.multiple_of(i * 32, 32), 32)
        total = acc[0, rows, :]
        for s in range(7):
            total = total + rs_recv[s, rows, :].astype(F32)
        mixed[rows, :] = (resid[rows, :].astype(F32) + total * scales[3]).astype(BF)
        return carry

    lax.fori_loop(0, ROWS // 32, finish, 0)

    for copy in sums + sent_w + sent_o:
        copy.wait_send()


def shards(
    hidden_in,
    ln_gain,
    q_gain,
    k_gain,
    w_query,
    w_key,
    w_value,
    w_out,
    cache_keys,
    cache_values,
    cache_lengths,
    amax_history,
    cycle_pos,
):
    half_dim = HEAD_DIM // 2
    inverse = rope_base ** (-(2.0 * np.arange(half_dim)) / HEAD_DIM)
    freq = jnp.asarray(np.concatenate([inverse, inverse])[None, :], F32)
    vmem = pl.BlockSpec(memory_space=pltpu.VMEM)
    smem = pl.BlockSpec(memory_space=pltpu.SMEM)
    hbm = pl.BlockSpec(memory_space=pl.ANY)
    dma = pltpu.SemaphoreType.DMA
    mixed, new_history = pl.pallas_call(
        kernel,
        out_shape=(
            jax.ShapeDtypeStruct((ROWS, HALF), BF),
            jax.ShapeDtypeStruct((4, HIST), F32),
        ),
        in_specs=[hbm, vmem, vmem, vmem, vmem, vmem, vmem, vmem, hbm, hbm, vmem, vmem, smem]
        + [vmem] * 3,
        out_specs=(vmem, vmem),
        scratch_shapes=[
            pltpu.VMEM((SPOTS, ROWS, HALF), BF),
            pltpu.VMEM((SEQS, CACHE, HEAD_DIM), BF),
            pltpu.VMEM((SEQS, CACHE, HEAD_DIM), BF),
            pltpu.VMEM((TPS, PACKED, HALF), BF),
            pltpu.VMEM((REPS, TPS, PACKED, HALF), BF),
            pltpu.VMEM((REPS, 512, HALF), BF),
            pltpu.VMEM((1024, 384), BF),
            pltpu.VMEM((512, 384), BF),
            pltpu.VMEM((16, 128), BF),
            pltpu.VMEM((2, ROWS, HALF), F32),
            pltpu.VMEM((ROWS, Q_LOCAL), F32),
            pltpu.VMEM((ROWS, Q_LOCAL), BF),
            pltpu.VMEM((7, ROWS, HALF), BF),
            pltpu.VMEM((7, ROWS, HALF), BF),
            pltpu.VMEM((ROWS, HALF), BF),
            pltpu.VMEM((6, 8, 128), F32),
            pltpu.VMEM((12, 8, 128), F32),
            dma((12,)),
            dma((7,)),
            dma((7,)),
            dma((30,)),
            dma((REPS, 2)),
            dma((30,)),
            dma((REPS, 2)),
            dma(()),
            dma(()),
            dma((7,)),
            dma((7,)),
            dma((12,)),
            dma((12,)),
        ],
        compiler_params=pltpu.CompilerParams(
            collective_id=0, has_side_effects=True, vmem_limit_bytes=62 * 2**20
        ),
        cost_estimate=pl.CostEstimate(
            flops=13 * 10**9, bytes_accessed=13 * 10**6, transcendentals=10**6
        ),
    )(
        hidden_in.reshape(ROWS, D),
        ln_gain.reshape(1, D),
        q_gain.reshape(1, HEAD_DIM),
        k_gain.reshape(1, HEAD_DIM),
        w_query,
        w_key,
        w_value,
        w_out,
        cache_keys,
        cache_values,
        cache_lengths.reshape(SEQS, 1),
        amax_history,
        cycle_pos,
        jnp.asarray(spread_matrices(), BF),
        jnp.asarray(join_matrices(), BF),
        freq,
    )
    return mixed.reshape(STEPS, SEQS, HALF), new_history


def solution(mesh):
    placed = (
        P(None, "rep", None),
        P(),
        P(),
        P(),
        P(("rep", "tp"), None),
        P(("rep", "tp"), None),
        P(("rep", "tp"), None),
        P("tp", "rep"),
        P("rep", None, "tp"),
        P("rep", None, "tp"),
        P("rep"),
        P(),
        P(),
    )
    return jax.shard_map(
        shards, mesh=mesh, in_specs=placed, out_specs=(P(None, "rep", "tp"), P()), check_vma=False
    )
```

```python
import jax
import jax.numpy as jnp
import numpy as np
from jax import lax
from jax.experimental import pallas as pl
from jax.experimental.pallas import tpu as pltpu
from jax.sharding import PartitionSpec as P

D = 5120
HEADS = 64
KV_HEADS = 8
HEAD_DIM = 128
STEPS = 4
HIST = 16
WINDOW = 8
Q_WIDTH = 8192
CACHE = 64
SEQS = 128
ROWS = STEPS * SEQS
REPS = 16
TPS = 8
SPOTS = 8
SHARD = 40
Q_LOCAL = 1024
HALF = 640
PACKED = 80
OUT_SHARD = 320
W_PIECES = ((0, 3), (3, 2), (5, 1), (6, 2))
O_PIECES = ((0, 160), (160, 160))

fp8_top = 448.0
rope_base = 1000000.0
norm_eps = 1e-06

BF = jnp.bfloat16
F32 = jnp.float32
MESH = pl.DeviceIdType.MESH


def dot(a, b):
    return jnp.dot(a, b, preferred_element_type=F32)


def quantize(weight, factor):
    return jnp.clip(weight.astype(F32) / factor, -fp8_top, fp8_top)


def kernel(
    hidden,
    ln_gain,
    q_gain,
    k_gain,
    w_query,
    w_key,
    w_value,
    w_out,
    cache_keys,
    cache_values,
    lengths,
    history,
    cycle,
    freq,
    mixed,
    new_history,
    rows_in,
    keys_in,
    values_in,
    stage,
    wbuf,
    obuf,
    spread,
    xs,
    tables,
    seq_len,
    acc,
    own_hi,
    attb,
    rs_recv,
    resid,
    amax_out,
    amax_in,
    local_sem,
    a2a_s,
    a2a_r,
    w_s,
    w_r,
    o_s,
    o_r,
    rs_s,
    rs_r,
    am_s,
    am_r,
):
    rep = lax.axis_index("rep")
    tp = lax.axis_index("tp")
    yh = rep // 8
    zz = (rep // 2) % 4
    core = rep % 2
    spot = rep // 2

    def rep_of(dy, dz, flip):
        return ((yh + dy) % 2) * 8 + ((zz + dz) % 4) * 2 + (core + flip) % 2

    def spot_of(dy, dz):
        return ((yh + dy) % 2) * 4 + (zz + dz) % 4

    def at_rep(index):
        return {"rep": index, "tp": tp}

    def at_tp(index):
        return {"rep": rep, "tp": index}

    peers = [(tp + s) % TPS for s in range(1, TPS)]
    y_far = rep_of(1, 0, 0)
    z_up = rep_of(0, 1, 0)
    z_down = rep_of(0, 3, 0)
    sibling = rep_of(0, 0, 1)
    line_x = tp // 2
    line_y = tp % 2

    loads = []
    for i in range(SPOTS):
        loads.append(
            pltpu.make_async_copy(hidden.at[:, pl.ds(i * HALF, HALF)], rows_in.at[i], local_sem.at[i])
        )
    loads.append(pltpu.make_async_copy(cache_keys, keys_in, local_sem.at[8]))
    loads.append(pltpu.make_async_copy(cache_values, values_in, local_sem.at[9]))
    loads.append(
        pltpu.make_async_copy(
            hidden.at[:, pl.ds(pl.multiple_of(tp * HALF, 128), HALF)], resid, local_sem.at[10]
        )
    )
    for load in loads:
        load.start()

    barrier = pltpu.get_barrier_semaphore()
    for peer in peers:
        pl.semaphore_signal(barrier, inc=1, device_id=at_tp(peer), device_id_type=MESH)
    for other in (y_far, z_up, z_down, sibling):
        pl.semaphore_signal(barrier, inc=1, device_id=at_rep(other), device_id_type=MESH)

    slot = lax.broadcasted_iota(jnp.int32, (1, HIST), 1)
    fans = (D, D, D, Q_WIDTH)
    roots = [float(np.sqrt(np.float32(fan))) for fan in fans]
    scales = []
    for m in range(4):
        behind = jnp.bitwise_and(cycle[m] + (2 * HIST - 1) - slot, HIST - 1)
        limit = jnp.max(
            jnp.where(behind < WINDOW, history[m : m + 1, :], 0.0), axis=1, keepdims=True
        )
        scales.append(limit / (fp8_top * roots[m]))

    def pack(j, tops):
        query = w_query[:, pl.ds(pl.multiple_of(j * Q_LOCAL, 128), Q_LOCAL)]
        key = w_key[:, pl.ds(pl.multiple_of(j * 128, 128), 128)]
        value = w_value[:, pl.ds(pl.multiple_of(j * 128, 128), 128)]
        q0 = quantize(query, scales[0])
        k0 = quantize(key, scales[1])
        v0 = quantize(value, scales[2])
        first = q0[:, :HALF]
        second = jnp.concatenate([q0[:, HALF:], k0, v0], axis=1)
        stage[j, 0:32, :] = first[0:32].astype(BF)
        stage[j, 32:48, :] = jnp.concatenate([first[32:40], second[32:40]], axis=0).astype(BF)
        stage[j, 48:80, :] = second[0:32].astype(BF)

        def top(values, old):
            found = jnp.max(jnp.abs(values.astype(F32)), axis=0, keepdims=True)
            for i in range(values.shape[1] // 128):
                old = jnp.maximum(old, found[:, i * 128 : (i + 1) * 128])
            return old

        return top(query, tops[0]), top(key, tops[1]), top(value, tops[2])

    none = jnp.zeros((1, 128), F32)
    tops = lax.fori_loop(0, TPS, pack, (none, none, none))

    pl.semaphore_wait(barrier, 11)

    a2a = []
    for s, peer in enumerate(peers):
        a2a.append(
            pltpu.make_async_remote_copy(
                src_ref=stage.at[peer],
                dst_ref=wbuf.at[rep, tp],
                send_sem=a2a_s.at[s],
                recv_sem=a2a_r.at[s],
                device_id=at_tp(peer),
                device_id_type=MESH,
            )
        )
    for copy in a2a:
        copy.start()
    own_plane = pltpu.make_async_copy(stage.at[tp], wbuf.at[rep, tp], local_sem.at[11])
    own_plane.start()

    def pack_out(i, old):
        rows = pl.ds(pl.multiple_of(i * 32, 32), 32)
        shard = w_out[rows, :]
        obuf[rep, rows, :] = quantize(shard, scales[3]).astype(BF)
        found = jnp.max(jnp.abs(shard.astype(F32)), axis=0, keepdims=True)
        return jnp.maximum(old, jnp.max(found, axis=1, keepdims=True))

    top_out = lax.fori_loop(0, OUT_SHARD // 32, pack_out, jnp.zeros((1, 1), F32))

    tile_row = lax.broadcasted_iota(jnp.int32, (8, 128), 0)
    found = [jnp.max(top, axis=1, keepdims=True) for top in tops] + [top_out]
    tile = jnp.zeros((8, 128), F32)
    for m in range(4):
        tile = jnp.where(tile_row == m, found[m], tile)
    amax_out[0] = tile

    def send_amax(stage_index, slot_index, where):
        return pltpu.make_async_remote_copy(
            src_ref=amax_out.at[stage_index],
            dst_ref=amax_in.at[slot_index],
            send_sem=am_s.at[slot_index],
            recv_sem=am_r.at[slot_index],
            device_id=where,
            device_id_type=MESH,
        )

    am_tp = [send_amax(0, s, at_tp(peer)) for s, peer in enumerate(peers)]
    am_y = [send_amax(1, 7, at_rep(y_far))]
    am_z = [send_amax(2, 8, at_rep(z_up)), send_amax(2, 9, at_rep(z_down))]
    am_w = [send_amax(3, 10, at_rep(z_up))]
    am_c = [send_amax(4, 11, at_rep(sibling))]

    def fold(copies, index, slots):
        for copy in copies:
            copy.wait()
        total = amax_out[index]
        for where in slots:
            total = jnp.maximum(total, amax_in[where])
        amax_out[index + 1] = total

    for copy in am_tp:
        copy.start()

    for load in loads[:8]:
        load.wait()

    def norm(i, carry):
        rows = pl.ds(pl.multiple_of(i * 32, 32), 32)
        parts = [rows_in[j, rows, :].astype(F32) for j in range(SPOTS)]
        square = parts[0] * parts[0]
        for part in parts[1:]:
            square = square + part * part
        mean = jnp.sum(square, axis=1, keepdims=True) / D
        factor = lax.rsqrt(mean + norm_eps)
        for j in range(SPOTS):
            gain = ln_gain[0:1, j * HALF : (j + 1) * HALF]
            rows_in[j, rows, :] = (parts[j] * factor * gain).astype(BF)
        return carry

    lax.fori_loop(0, ROWS // 32, norm, 0)

    def relay(buf, pieces, send_sem, recv_sem):
        sent = []

        def send(block, piece, *targets):
            view = buf.at[block, pl.ds(*pieces[piece])]
            for target in targets:
                copy = pltpu.make_async_remote_copy(
                    src_ref=view,
                    dst_ref=view,
                    send_sem=send_sem.at[len(sent)],
                    recv_sem=recv_sem.at[block, piece],
                    device_id=at_rep(target),
                    device_id_type=MESH,
                )
                copy.start()
                sent.append(copy)

        def arrive(block, *which):
            for piece in which or range(len(pieces)):
                view = buf.at[block, pl.ds(*pieces[piece])]
                pltpu.make_async_remote_copy(
                    src_ref=view,
                    dst_ref=view,
                    send_sem=send_sem.at[0],
                    recv_sem=recv_sem.at[block, piece],
                    device_id=at_rep(sibling),
                    device_id_type=MESH,
                ).wait_recv()

        return send, arrive, sent

    send_w, arrive_w, sent_w = relay(wbuf, W_PIECES, w_s, w_r)
    send_o, arrive_o, sent_o = relay(obuf, O_PIECES, o_s, o_r)

    def both_w(dy, dz):
        arrive_w(rep_of(dy, dz, 1))

    def both_o(dy, dz):
        arrive_o(rep_of(dy, dz, 1))

    def far_o():
        for piece in range(2):
            arrive_o(y_far, piece)
            send_o(y_far, piece, z_up, z_down, sibling)

    def beside_o(dy):
        for piece in range(2):
            for dz, target, keep in ((1, z_down, 0), (3, z_up, 1)):
                block = rep_of(dy, dz, 0)
                arrive_o(block, piece)
                if piece == keep:
                    send_o(block, piece, target)
                send_o(block, piece, sibling)

    def across_o(dy):
        for piece in range(2):
            arrive_o(rep_of(dy, 2, 0), piece)
            send_o(rep_of(dy, 2, 0), piece, sibling)

    for piece in range(2):
        send_o(rep, piece, z_up, z_down, y_far, sibling)

    diagonal = lax.broadcasted_iota(jnp.int32, (SEQS, SEQS), 0) == lax.broadcasted_iota(
        jnp.int32, (SEQS, SEQS), 1
    )
    seq_len[...] = jnp.sum(
        jnp.where(diagonal, lengths[...].astype(F32), 0.0), axis=1, keepdims=True
    )
    lane = lax.broadcasted_iota(jnp.int32, (SEQS, HEAD_DIM), 1)

    def turn(s, carry):
        rows = pl.ds(pl.multiple_of(s * SEQS, SEQS), SEQS)
        angles = (seq_len[...] + lax.convert_element_type(s, F32)) * freq[...]
        tables[0, rows, :] = jnp.cos(angles)
        sine = jnp.sin(angles)
        tables[1, rows, :] = jnp.where(lane < 64, -sine, sine)
        return carry

    column = lax.broadcasted_iota(jnp.int32, (1, 768), 1)
    block_of = jnp.right_shift(column * 1366, 16)
    inside = column - block_of * 48
    wanted = (
        jnp.where(inside < 40, block_of * SHARD + inside, -1),
        jnp.where(
            inside < 8,
            -1,
            block_of * SHARD + jnp.where(inside < 16, inside + 24, inside - 16),
        ),
    )
    for h in range(2):
        for part in range(5):
            row = lax.broadcasted_iota(jnp.int32, (128, 768), 0) + part * 128
            spread[h, part * 128 : (part + 1) * 128, :] = jnp.where(
                row == wanted[h], 1.0, 0.0
            ).astype(BF)

    lax.fori_loop(0, STEPS, turn, 0)
    own_plane.wait()
    for copy in a2a:
        copy.wait()

    send_w(rep, 0, y_far)
    send_w(rep, 1, y_far)
    send_w(rep, 2, z_up, z_down, sibling)
    send_w(rep, 3, z_up, z_down, sibling)
    send_w(rep, 0, z_up, z_down, sibling)
    send_w(rep, 1, z_up, z_down, sibling)
    send_w(rep, 2, y_far)
    send_w(rep, 3, y_far)

    acc[...] = jnp.zeros_like(acc)

    def select(dy, dz):
        place = spot_of(dy, dz)

        def tiles(i, carry):
            rows = pl.ds(pl.multiple_of(i * 256, 256), 256)
            for h in range(2):
                xs[place, h, rows, :] = dot(rows_in[place, rows, :], spread[h]).astype(BF)
            return carry

        lax.fori_loop(0, 2, tiles, 0)

    def project(dy, dz):
        place = spot_of(dy, dz)

        def tiles(i, carry):
            rows = pl.ds(pl.multiple_of(i * 256, 256), 256)
            for h in range(2):
                block = wbuf[pl.ds(place * 2, 2), :, h * 32 : h * 32 + 48, :].reshape(768, HALF)
                acc[h, rows, :] = acc[h, rows, :] + dot(xs[place, h, rows, :], block)
            return carry

        lax.fori_loop(0, 2, tiles, 0)

    select(0, 0)
    select(1, 0)
    for piece in (2, 3):
        for dz, target, keep in ((1, z_down, 2), (3, z_up, 3)):
            block = rep_of(0, dz, 0)
            arrive_w(block, piece)
            if piece == keep:
                send_w(block, piece, target)
            send_w(block, piece, y_far, sibling)
    select(0, 1)
    for piece in (0, 1):
        arrive_w(y_far, piece)
        send_w(y_far, piece, z_up, z_down, sibling)
    both_w(0, 0)
    project(0, 0)
    select(0, 3)
    fold(am_tp, 0, range(7))
    am_y[0].start()
    for piece in (0, 1):
        for dz, target, keep in ((1, z_down, 0), (3, z_up, 1)):
            block = rep_of(0, dz, 0)
            arrive_w(block, piece)
            if piece == keep:
                send_w(block, piece, target)
            send_w(block, piece, sibling)
    for piece in (2, 3):
        arrive_w(y_far, piece)
        send_w(y_far, piece, sibling)
    both_w(0, 1)
    project(0, 1)
    select(1, 1)
    for piece in (2, 3):
        arrive_w(rep_of(0, 2, 0), piece)
        send_w(rep_of(0, 2, 0), piece, y_far, sibling)
    both_w(0, 3)
    project(0, 3)
    both_w(1, 0)
    project(1, 0)
    select(1, 3)
    fold(am_y, 1, [7])
    for copy in am_z:
        copy.start()
    for piece in (2, 3):
        for dz in (1, 3):
            arrive_w(rep_of(1, dz, 0), piece)
            send_w(rep_of(1, dz, 0), piece, sibling)
    select(0, 2)
    for piece in (0, 1):
        for dz, target, keep in ((1, z_down, 0), (3, z_up, 1)):
            block = rep_of(1, dz, 0)
            arrive_w(block, piece)
            if piece == keep:
                send_w(block, piece, target)
            send_w(block, piece, sibling)
    select(1, 2)
    both_w(1, 1)
    project(1, 1)
    fold(am_z, 2, [8, 9])
    am_w[0].start()
    for piece in (0, 1):
        arrive_w(rep_of(0, 2, 0), piece)
        send_w(rep_of(0, 2, 0), piece, sibling)
    far_o()
    beside_o(0)
    both_w(1, 3)
    project(1, 3)
    both_w(0, 2)
    project(0, 2)
    fold(am_w, 3, [10])
    am_c[0].start()
    for piece in (2, 3, 0, 1):
        arrive_w(rep_of(1, 2, 0), piece)
        send_w(rep_of(1, 2, 0), piece, sibling)
    both_w(1, 2)
    project(1, 2)

    def head_norm(s, carry):
        rows = pl.ds(pl.multiple_of(s * SEQS, SEQS), SEQS)
        cosine = tables[0, rows, :]
        sine = tables[1, rows, :]
        for head in range(9):
            h, lanes = (0, head) if head < 5 else (1, head - 5)
            cols = pl.ds(lanes * HEAD_DIM, HEAD_DIM)
            values = acc[h, rows, cols]
            gain = q_gain[...] if head < 8 else k_gain[...]
            mean = jnp.sum(values * values, axis=1, keepdims=True) / HEAD_DIM
            values = values * lax.rsqrt(mean + norm_eps) * gain
            acc[h, rows, cols] = values * cosine + pltpu.roll(values, 64, 1) * sine
        cols = pl.ds(512, HEAD_DIM)
        acc[1, rows, cols] = acc[1, rows, cols] * scales[2]
        return carry

    lax.fori_loop(0, STEPS, head_norm, 0)

    for load in loads[8:]:
        load.wait()

    old_seq = lax.broadcasted_iota(jnp.int32, (8, 8 * CACHE), 0)
    old_col = lax.broadcasted_iota(jnp.int32, (8, 8 * CACHE), 1)
    old_slot = jnp.where(
        jnp.right_shift(old_col, 6) == old_seq, jnp.bitwise_and(old_col, CACHE - 1), CACHE
    ).astype(F32)
    new_row = lax.broadcasted_iota(jnp.int32, (32, 32), 0)
    new_col = lax.broadcasted_iota(jnp.int32, (32, 32), 1)
    new_live = (jnp.bitwise_and(new_row, 7) == jnp.bitwise_and(new_col, 7)) & (
        jnp.right_shift(new_col, 3) <= jnp.right_shift(new_row, 3)
    )
    new_bias = jnp.where(new_live, 0.0, -1e30)
    scaling = HEAD_DIM ** (-0.5)
    nt = (((1,), (1,)), ((), ()))

    def attend_eight(g):
        seqs = pl.ds(pl.multiple_of(g * 8, 8), 8)

        def pick(h, lanes):
            return [
                acc[h, pl.ds(pl.multiple_of(s * SEQS + g * 8, 8), 8), pl.ds(lanes * HEAD_DIM, HEAD_DIM)]
                for s in range(STEPS)
            ]

        rows = []
        for head in range(8):
            rows += pick(0, head) if head < 5 else pick(1, head - 5)
        queries = jnp.concatenate(rows, axis=0).astype(BF)
        fresh_keys = jnp.concatenate(pick(1, 3), axis=0).astype(BF)
        fresh_values = jnp.concatenate(pick(1, 4), axis=0).astype(BF)
        old_keys = keys_in[seqs].reshape(8 * CACHE, HEAD_DIM)
        old_values = values_in[seqs].reshape(8 * CACHE, HEAD_DIM)
        old_bias = jnp.where(old_slot < seq_len[seqs, :], 0.0, -1e30)
        old = lax.dot_general(queries, old_keys, nt, preferred_element_type=F32)
        new = lax.dot_general(queries, fresh_keys, nt, preferred_element_type=F32)
        old = (old.reshape(32, 8, 8 * CACHE) * scaling + old_bias[None]).reshape(256, 8 * CACHE)
        new = (new.reshape(8, 32, 32) * scaling + new_bias[None]).reshape(256, 32)
        top = jnp.maximum(
            jnp.max(old, axis=1, keepdims=True), jnp.max(new, axis=1, keepdims=True)
        )
        old = jnp.exp(old - top)
        new = jnp.exp(new - top)
        total = jnp.sum(old, axis=1, keepdims=True) + jnp.sum(new, axis=1, keepdims=True)
        result = dot(old.astype(BF), old_values) + dot(new.astype(BF), fresh_values)
        return result / total

    def attend(g, carry):
        low = attend_eight(g * 2)
        high = attend_eight(g * 2 + 1)
        for head in range(8):
            for s in range(STEPS):
                start = head * 32 + s * 8
                pair = jnp.concatenate([low[start : start + 8], high[start : start + 8]], axis=0)
                attb[
                    pl.ds(pl.multiple_of(s * SEQS + g * 16, 16), 16),
                    pl.ds(head * HEAD_DIM, HEAD_DIM),
                ] = pair.astype(BF)
        return carry

    lax.fori_loop(0, SEQS // 16, attend, 0)

    beside_o(1)
    for dy in range(2):
        for dz in (1, 3):
            both_o(dy, dz)

    lo = pl.ds(0, 256)
    hi = pl.ds(256, 256)

    def slot_of(index):
        return rows_in.at[index // 2, pl.ds((index % 2) * 256, 256)]

    def push(index, target):
        return pltpu.make_async_remote_copy(
            src_ref=slot_of(index),
            dst_ref=rs_recv.at[index],
            send_sem=rs_s.at[index],
            recv_sem=rs_r.at[index],
            device_id=at_tp(target),
            device_id_type=MESH,
        )

    def put(index, values):
        rows_in[index // 2, pl.ds((index % 2) * 256, 256), :] = values.astype(BF)

    across_x = [((line_x + k) % 4) * 2 + line_y for k in range(4)]
    y_mate = line_x * 2 + 1 - line_y
    to_mate = [push(k, y_mate) for k in range(4)]
    other_x = [push(3 + k, across_x[k]) for k in range(1, 4)]
    this_hi = [push(6 + k, across_x[k]) for k in range(1, 4)]
    this_lo = [push(9 + k, across_x[k]) for k in range(1, 4)]
    last = push(13, y_mate)

    def partial(k, row, rows):
        owner = ((line_x + k) % 4) * 2 + row
        weights = obuf[pl.ds(owner * 2, 2)].reshape(HALF, Q_LOCAL)
        return lax.dot_general(attb[rows, :], weights, nt, preferred_element_type=F32)

    def other_row():
        for k in (1, 2, 3, 0):
            put(k, partial(k, 1 - line_y, lo))
            to_mate[k].start()
            values = partial(k, 1 - line_y, hi)
            if k:
                put(3 + k, values)
                other_x[k - 1].start()
            else:
                own_hi[0] = values

    def this_row():
        for k in (1, 2, 3, 0):
            values = partial(k, line_y, hi)
            if k:
                put(6 + k, values)
                this_hi[k - 1].start()
            else:
                own_hi[1] = values
            acc[k // 2, pl.ds((k % 2) * 256, 256), :] = partial(k, line_y, lo)

    other_first = (zz + 1) % 2 == 1 - line_y
    pl.when(other_first)(other_row)
    pl.when(jnp.logical_not(other_first))(this_row)
    across_o(0)
    across_o(1)
    for dy in range(2):
        for dz in (0, 2):
            both_o(dy, dz)
    pl.when(other_first)(this_row)
    pl.when(jnp.logical_not(other_first))(other_row)

    for k in (1, 2, 3):
        to_mate[k].wait_recv()
        put(9 + k, acc[k // 2, pl.ds((k % 2) * 256, 256), :] + rs_recv[k].astype(F32))
        this_lo[k - 1].start()
    for copy in other_x:
        copy.wait_recv()
    total = own_hi[0]
    for k in (1, 2, 3):
        total = total + rs_recv[3 + k].astype(F32)
    put(13, total)
    last.start()
    to_mate[0].wait_recv()

    def finish(first, gathered, base):
        def step(i, carry):
            rows = pl.ds(pl.multiple_of(i * 32, 32), 32)
            outs = pl.ds(pl.multiple_of(first + i * 32, 32), 32)
            total = base[rows, :]
            for index in gathered:
                total = total + rs_recv[index, rows, :].astype(F32)
            mixed[outs, :] = (resid[outs, :].astype(F32) + total * scales[3]).astype(BF)
            return carry

        lax.fori_loop(0, 8, step, 0)

    for copy in this_lo:
        copy.wait_recv()
    finish(0, (0, 10, 11, 12), acc.at[0])
    for copy in this_hi:
        copy.wait_recv()
    last.wait_recv()
    finish(256, (7, 8, 9, 13), own_hi.at[1])

    for copy in to_mate + other_x + this_hi + this_lo + [last] + sent_w + sent_o:
        copy.wait_send()
    fold(am_c, 4, [11])
    for m in range(4):
        new_history[m : m + 1, :] = jnp.where(
            slot == cycle[m],
            amax_out[5, m : m + 1, 0:1] * roots[m],
            history[m : m + 1, :],
        )


def shards(
    hidden_in,
    ln_gain,
    q_gain,
    k_gain,
    w_query,
    w_key,
    w_value,
    w_out,
    cache_keys,
    cache_values,
    cache_lengths,
    amax_history,
    cycle_pos,
):
    half_dim = HEAD_DIM // 2
    inverse = rope_base ** (-(2.0 * np.arange(half_dim)) / HEAD_DIM)
    freq = jnp.asarray(np.concatenate([inverse, inverse])[None, :], F32)
    vmem = pl.BlockSpec(memory_space=pltpu.VMEM)
    smem = pl.BlockSpec(memory_space=pltpu.SMEM)
    hbm = pl.BlockSpec(memory_space=pl.ANY)
    dma = pltpu.SemaphoreType.DMA
    mixed, new_history = pl.pallas_call(
        kernel,
        out_shape=(
            jax.ShapeDtypeStruct((ROWS, HALF), BF),
            jax.ShapeDtypeStruct((4, HIST), F32),
        ),
        in_specs=[hbm, vmem, vmem, vmem, vmem, vmem, vmem, vmem, hbm, hbm, vmem, vmem, smem]
        + [vmem],
        out_specs=(vmem, vmem),
        scratch_shapes=[
            pltpu.VMEM((SPOTS, ROWS, HALF), BF),
            pltpu.VMEM((SEQS, CACHE, HEAD_DIM), BF),
            pltpu.VMEM((SEQS, CACHE, HEAD_DIM), BF),
            pltpu.VMEM((TPS, PACKED, HALF), BF),
            pltpu.VMEM((REPS, TPS, PACKED, HALF), BF),
            pltpu.VMEM((REPS, OUT_SHARD, Q_LOCAL), BF),
            pltpu.VMEM((2, HALF, 768), BF),
            pltpu.VMEM((SPOTS, 2, ROWS, 768), BF),
            pltpu.VMEM((2, ROWS, HEAD_DIM), F32),
            pltpu.VMEM((SEQS, 1), F32),
            pltpu.VMEM((2, ROWS, HALF), F32),
            pltpu.VMEM((2, 256, HALF), F32),
            pltpu.VMEM((ROWS, Q_LOCAL), BF),
            pltpu.VMEM((14, 256, HALF), BF),
            pltpu.VMEM((ROWS, HALF), BF),
            pltpu.VMEM((6, 8, 128), F32),
            pltpu.VMEM((12, 8, 128), F32),
            dma((12,)),
            dma((7,)),
            dma((7,)),
            dma((60,)),
            dma((REPS, 4)),
            dma((30,)),
            dma((REPS, 2)),
            dma((14,)),
            dma((14,)),
            dma((12,)),
            dma((12,)),
        ],
        compiler_params=pltpu.CompilerParams(
            collective_id=0, has_side_effects=True, vmem_limit_bytes=62 * 2**20
        ),
        cost_estimate=pl.CostEstimate(
            flops=13 * 10**9, bytes_accessed=13 * 10**6, transcendentals=10**6
        ),
    )(
        hidden_in.reshape(ROWS, D),
        ln_gain.reshape(1, D),
        q_gain.reshape(1, HEAD_DIM),
        k_gain.reshape(1, HEAD_DIM),
        w_query,
        w_key,
        w_value,
        w_out.T,
        cache_keys,
        cache_values,
        cache_lengths.reshape(1, SEQS),
        amax_history,
        cycle_pos,
        freq,
    )
    return mixed.reshape(STEPS, SEQS, HALF), new_history


def solution(mesh):
    placed = (
        P(None, "rep", None),
        P(),
        P(),
        P(),
        P(("rep", "tp"), None),
        P(("rep", "tp"), None),
        P(("rep", "tp"), None),
        P("tp", "rep"),
        P("rep", None, "tp"),
        P("rep", None, "tp"),
        P("rep"),
        P(),
        P(),
    )
    return jax.shard_map(
        shards, mesh=mesh, in_specs=placed, out_specs=(P(None, "rep", "tp"), P()), check_vma=False
    )
```

```python
import jax
import jax.numpy as jnp
import numpy as np
from jax import lax
from jax.experimental import pallas as pl
from jax.experimental.pallas import tpu as pltpu
from jax.sharding import PartitionSpec as P

D = 5120
HEADS = 64
KV_HEADS = 8
HEAD_DIM = 128
STEPS = 4
HIST = 16
WINDOW = 8
Q_WIDTH = 8192
CACHE = 64
SEQS = 128
ROWS = STEPS * SEQS
REPS = 16
TPS = 8
SPOTS = 8
SHARD = 40
Q_LOCAL = 1024
HALF = 640
PACKED = 80
OUT_SHARD = 320
LOW = 224
PLANES = ((0, 0), (0, 1), (1, 0), (3, 0), (1, 1), (3, 1), (2, 0), (2, 1))
W_PIECES = ((5, 3), (2, 3), (0, 1), (1, 1))
O_PIECES = ((0, 160), (160, 160))

fp8_top = 448.0
rope_base = 1000000.0
norm_eps = 1e-06

BF = jnp.bfloat16
F32 = jnp.float32
MESH = pl.DeviceIdType.MESH


def dot(a, b):
    return jnp.dot(a, b, preferred_element_type=F32)


def quantize(weight, factor):
    return jnp.clip(weight.astype(F32) / factor, -fp8_top, fp8_top)


def kernel(
    hidden,
    ln_gain,
    q_gain,
    k_gain,
    w_query,
    w_key,
    w_value,
    w_out,
    cache_keys,
    cache_values,
    lengths,
    history,
    cycle,
    freq,
    mixed,
    new_history,
    rows_in,
    keys_in,
    values_in,
    stage,
    wbuf,
    obuf,
    spread,
    xs,
    tables,
    seq_len,
    acc,
    attb,
    rs_recv,
    resid,
    amax_out,
    amax_in,
    local_sem,
    a2a_s,
    a2a_r,
    w_s,
    w_r,
    o_s,
    o_r,
    rs_s,
    rs_r,
    am_s,
    am_r,
):
    rep = lax.axis_index("rep")
    tp = lax.axis_index("tp")
    yh = rep // 8
    zz = (rep // 2) % 4
    core = rep % 2
    spot = rep // 2

    def rep_of(dy, dz, flip):
        return ((yh + dy) % 2) * 8 + ((zz + dz) % 4) * 2 + (core + flip) % 2

    def spot_of(dy, dz):
        return ((yh + dy) % 2) * 4 + (zz + dz) % 4

    def at_rep(index):
        return {"rep": index, "tp": tp}

    def at_tp(index):
        return {"rep": rep, "tp": index}

    y_far = rep_of(1, 0, 0)
    z_up = rep_of(0, 1, 0)
    z_down = rep_of(0, 3, 0)
    sibling = rep_of(0, 0, 1)
    line_x = tp // 2
    line_y = tp % 2
    peers = [((line_x + kx) % 4) * 2 + (line_y + ky) % 2 for kx, ky in PLANES[1:]]

    loads = []
    for i in range(SPOTS):
        loads.append(
            pltpu.make_async_copy(hidden.at[:, pl.ds(i * HALF, HALF)], rows_in.at[i], local_sem.at[i])
        )
    loads.append(pltpu.make_async_copy(cache_keys, keys_in, local_sem.at[8]))
    loads.append(pltpu.make_async_copy(cache_values, values_in, local_sem.at[9]))
    loads.append(
        pltpu.make_async_copy(
            hidden.at[:, pl.ds(pl.multiple_of(tp * HALF, 128), HALF)], resid, local_sem.at[10]
        )
    )
    for load in loads:
        load.start()

    barrier = pltpu.get_barrier_semaphore()
    for peer in peers:
        pl.semaphore_signal(barrier, inc=1, device_id=at_tp(peer), device_id_type=MESH)
    for other in (y_far, z_up, z_down, sibling):
        pl.semaphore_signal(barrier, inc=1, device_id=at_rep(other), device_id_type=MESH)

    slot = lax.broadcasted_iota(jnp.int32, (1, HIST), 1)
    fans = (D, D, D, Q_WIDTH)
    roots = [float(np.sqrt(np.float32(fan))) for fan in fans]
    scales = []
    for m in range(4):
        behind = jnp.bitwise_and(cycle[m] + (2 * HIST - 1) - slot, HIST - 1)
        limit = jnp.max(
            jnp.where(behind < WINDOW, history[m : m + 1, :], 0.0), axis=1, keepdims=True
        )
        scales.append(limit / (fp8_top * roots[m]))

    def pack(j, tops):
        query = w_query[:, pl.ds(pl.multiple_of(j * Q_LOCAL, 128), Q_LOCAL)]
        key = w_key[:, pl.ds(pl.multiple_of(j * 128, 128), 128)]
        value = w_value[:, pl.ds(pl.multiple_of(j * 128, 128), 128)]
        q0 = quantize(query, scales[0])
        k0 = quantize(key, scales[1])
        v0 = quantize(value, scales[2])
        first = q0[:, :HALF]
        second = jnp.concatenate([q0[:, HALF:], k0, v0], axis=1)
        stage[j, 0:32, :] = first[0:32].astype(BF)
        stage[j, 32:48, :] = jnp.concatenate([first[32:40], second[32:40]], axis=0).astype(BF)
        stage[j, 48:80, :] = second[0:32].astype(BF)

        def top(values, old):
            found = jnp.max(jnp.abs(values.astype(F32)), axis=0, keepdims=True)
            for i in range(values.shape[1] // 128):
                old = jnp.maximum(old, found[:, i * 128 : (i + 1) * 128])
            return old

        return top(query, tops[0]), top(key, tops[1]), top(value, tops[2])

    none = jnp.zeros((1, 128), F32)
    tops = lax.fori_loop(0, TPS, pack, (none, none, none))

    pl.semaphore_wait(barrier, 11)

    a2a = []
    for s, peer in enumerate(peers):
        a2a.append(
            pltpu.make_async_remote_copy(
                src_ref=stage.at[peer],
                dst_ref=wbuf.at[rep, s + 1],
                send_sem=a2a_s.at[s],
                recv_sem=a2a_r.at[s],
                device_id=at_tp(peer),
                device_id_type=MESH,
            )
        )
    for copy in a2a:
        copy.start()
    own_plane = pltpu.make_async_copy(stage.at[tp], wbuf.at[rep, 0], local_sem.at[11])
    own_plane.start()

    def relay(buf, pieces, send_sem, recv_sem):
        sent = []

        def send(block, piece, *targets):
            view = buf.at[block, pl.ds(*pieces[piece])]
            for target in targets:
                copy = pltpu.make_async_remote_copy(
                    src_ref=view,
                    dst_ref=view,
                    send_sem=send_sem.at[len(sent)],
                    recv_sem=recv_sem.at[block, piece],
                    device_id=at_rep(target),
                    device_id_type=MESH,
                )
                copy.start()
                sent.append(copy)

        def arrive(block, *which):
            for piece in which or range(len(pieces)):
                view = buf.at[block, pl.ds(*pieces[piece])]
                pltpu.make_async_remote_copy(
                    src_ref=view,
                    dst_ref=view,
                    send_sem=send_sem.at[0],
                    recv_sem=recv_sem.at[block, piece],
                    device_id=at_rep(sibling),
                    device_id_type=MESH,
                ).wait_recv()

        return send, arrive, sent

    send_w, arrive_w, sent_w = relay(wbuf, W_PIECES, w_s, w_r)
    send_o, arrive_o, sent_o = relay(obuf, O_PIECES, o_s, o_r)

    def both_w(dy, dz):
        arrive_w(rep_of(dy, dz, 1))

    def both_o(dy, dz):
        arrive_o(rep_of(dy, dz, 1))

    def far_o():
        for piece in range(2):
            arrive_o(y_far, piece)
            send_o(y_far, piece, z_up, z_down, sibling)

    def beside_o(dy):
        for piece in range(2):
            for dz, target, keep in ((1, z_down, 0), (3, z_up, 1)):
                block = rep_of(dy, dz, 0)
                arrive_o(block, piece)
                if piece == keep:
                    send_o(block, piece, target)
                send_o(block, piece, sibling)

    def across_o(dy):
        for piece in range(2):
            arrive_o(rep_of(dy, 2, 0), piece)
            send_o(rep_of(dy, 2, 0), piece, sibling)

    own_plane.wait()
    send_w(rep, 2, z_up, z_down, y_far, sibling)

    def pack_out(i, old):
        rows = pl.ds(pl.multiple_of(i * 32, 32), 32)
        shard = w_out[rows, :]
        obuf[rep, rows, :] = quantize(shard, scales[3]).astype(BF)
        found = jnp.max(jnp.abs(shard.astype(F32)), axis=0, keepdims=True)
        return jnp.maximum(old, jnp.max(found, axis=1, keepdims=True))

    top_out = lax.fori_loop(0, OUT_SHARD // 32, pack_out, jnp.zeros((1, 1), F32))

    a2a[0].wait_recv()
    send_w(rep, 3, z_up, z_down, y_far, sibling)
    for piece in range(2):
        send_o(rep, piece, z_up, z_down, sibling)

    tile_row = lax.broadcasted_iota(jnp.int32, (8, 128), 0)
    found = [jnp.max(top, axis=1, keepdims=True) for top in tops] + [top_out]
    tile = jnp.zeros((8, 128), F32)
    for m in range(4):
        tile = jnp.where(tile_row == m, found[m], tile)
    amax_out[0] = tile

    def send_amax(stage_index, slot_index, where):
        return pltpu.make_async_remote_copy(
            src_ref=amax_out.at[stage_index],
            dst_ref=amax_in.at[slot_index],
            send_sem=am_s.at[slot_index],
            recv_sem=am_r.at[slot_index],
            device_id=where,
            device_id_type=MESH,
        )

    am_tp = [send_amax(0, s, at_tp(peer)) for s, peer in enumerate(peers)]
    am_y = [send_amax(1, 7, at_rep(y_far))]
    am_z = [send_amax(2, 8, at_rep(z_up)), send_amax(2, 9, at_rep(z_down))]
    am_w = [send_amax(3, 10, at_rep(z_up))]
    am_c = [send_amax(4, 11, at_rep(sibling))]

    def fold(copies, index, slots):
        for copy in copies:
            copy.wait()
        total = amax_out[index]
        for where in slots:
            total = jnp.maximum(total, amax_in[where])
        amax_out[index + 1] = total

    for copy in am_tp:
        copy.start()

    for load in loads[:8]:
        load.wait()

    def norm(i, carry):
        rows = pl.ds(pl.multiple_of(i * 32, 32), 32)
        parts = [rows_in[j, rows, :].astype(F32) for j in range(SPOTS)]
        square = parts[0] * parts[0]
        for part in parts[1:]:
            square = square + part * part
        mean = jnp.sum(square, axis=1, keepdims=True) / D
        factor = lax.rsqrt(mean + norm_eps)
        for j in range(SPOTS):
            gain = ln_gain[0:1, j * HALF : (j + 1) * HALF]
            rows_in[j, rows, :] = (parts[j] * factor * gain).astype(BF)
        return carry

    for copy in a2a[1:4]:
        copy.wait_recv()
    send_w(rep, 1, y_far, z_up, z_down, sibling)
    def beside_first(piece):
        for dz, target, keep in ((1, z_down, 2), (3, z_up, 3)):
            block = rep_of(0, dz, 0)
            arrive_w(block, piece)
            if piece == keep:
                send_w(block, piece, target)
            send_w(block, piece, y_far, sibling)

    beside_first(2)
    for copy in a2a[4:]:
        copy.wait_recv()
    send_w(rep, 0, y_far, z_up, z_down, sibling)
    beside_first(3)
    for piece in range(2):
        send_o(rep, piece, y_far)
    lax.fori_loop(0, ROWS // 32, norm, 0)

    diagonal = lax.broadcasted_iota(jnp.int32, (SEQS, SEQS), 0) == lax.broadcasted_iota(
        jnp.int32, (SEQS, SEQS), 1
    )
    seq_len[...] = jnp.sum(
        jnp.where(diagonal, lengths[...].astype(F32), 0.0), axis=1, keepdims=True
    )
    lane = lax.broadcasted_iota(jnp.int32, (SEQS, HEAD_DIM), 1)

    def turn(s, carry):
        rows = pl.ds(pl.multiple_of(s * SEQS, SEQS), SEQS)
        angles = (seq_len[...] + lax.convert_element_type(s, F32)) * freq[...]
        tables[0, rows, :] = jnp.cos(angles)
        sine = jnp.sin(angles)
        tables[1, rows, :] = jnp.where(lane < 64, -sine, sine)
        return carry

    column = lax.broadcasted_iota(jnp.int32, (1, 768), 1)
    block_of = jnp.right_shift(column * 1366, 16)
    inside = column - block_of * 48
    plane = jnp.bitwise_and(block_of, 7)
    off_x = jnp.zeros_like(plane)
    off_y = jnp.zeros_like(plane)
    for n, (kx, ky) in enumerate(PLANES):
        off_x = jnp.where(plane == n, kx, off_x)
        off_y = jnp.where(plane == n, ky, off_y)
    block_of = (
        block_of
        - plane
        + jnp.bitwise_and(line_x + 4 - off_x, 3) * 2
        + jnp.bitwise_and(line_y + off_y, 1)
    )
    wanted = (
        jnp.where(inside < 40, block_of * SHARD + inside, -1),
        jnp.where(
            inside < 8,
            -1,
            block_of * SHARD + jnp.where(inside < 16, inside + 24, inside - 16),
        ),
    )
    for h in range(2):
        for part in range(5):
            row = lax.broadcasted_iota(jnp.int32, (128, 768), 0) + part * 128
            spread[h, part * 128 : (part + 1) * 128, :] = jnp.where(
                row == wanted[h], 1.0, 0.0
            ).astype(BF)

    lax.fori_loop(0, STEPS, turn, 0)

    acc[...] = jnp.zeros_like(acc)

    def select(dy, dz):
        place = spot_of(dy, dz)

        def tiles(i, carry):
            rows = pl.ds(pl.multiple_of(i * 256, 256), 256)
            for h in range(2):
                xs[place, h, rows, :] = dot(rows_in[place, rows, :], spread[h]).astype(BF)
            return carry

        lax.fori_loop(0, 2, tiles, 0)

    def project(dy, dz):
        place = spot_of(dy, dz)

        def tiles(i, carry):
            rows = pl.ds(pl.multiple_of(i * 256, 256), 256)
            for h in range(2):
                block = wbuf[pl.ds(place * 2, 2), :, h * 32 : h * 32 + 48, :].reshape(768, HALF)
                acc[h, rows, :] = acc[h, rows, :] + dot(xs[place, h, rows, :], block)
            return carry

        lax.fori_loop(0, 2, tiles, 0)

    select(0, 0)
    select(1, 0)
    select(0, 1)
    for piece in (1, 0):
        arrive_w(y_far, piece)
        send_w(y_far, piece, z_up, z_down, sibling)
    both_w(0, 0)
    project(0, 0)
    select(0, 3)
    fold(am_tp, 0, range(7))
    am_y[0].start()
    for piece in (1, 0):
        for dz, target, keep in ((1, z_down, 0), (3, z_up, 1)):
            block = rep_of(0, dz, 0)
            arrive_w(block, piece)
            if piece == keep:
                send_w(block, piece, target)
            send_w(block, piece, sibling)
    for piece in (2, 3):
        arrive_w(y_far, piece)
        send_w(y_far, piece, sibling)
    both_w(0, 1)
    project(0, 1)
    select(1, 1)
    for piece in (2, 3):
        arrive_w(rep_of(0, 2, 0), piece)
        send_w(rep_of(0, 2, 0), piece, y_far, sibling)
    both_w(0, 3)
    project(0, 3)
    both_w(1, 0)
    project(1, 0)
    select(1, 3)
    fold(am_y, 1, [7])
    for copy in am_z:
        copy.start()
    for piece in (2, 3):
        for dz in (1, 3):
            arrive_w(rep_of(1, dz, 0), piece)
            send_w(rep_of(1, dz, 0), piece, sibling)
    select(0, 2)
    for piece in (1, 0):
        for dz, target, keep in ((1, z_down, 0), (3, z_up, 1)):
            block = rep_of(1, dz, 0)
            arrive_w(block, piece)
            if piece == keep:
                send_w(block, piece, target)
            send_w(block, piece, sibling)
    select(1, 2)
    both_w(1, 1)
    project(1, 1)
    fold(am_z, 2, [8, 9])
    am_w[0].start()
    for piece in (1, 0):
        arrive_w(rep_of(0, 2, 0), piece)
        send_w(rep_of(0, 2, 0), piece, sibling)
    far_o()
    beside_o(0)
    both_w(1, 3)
    project(1, 3)
    both_w(0, 2)
    project(0, 2)
    fold(am_w, 3, [10])
    am_c[0].start()
    for piece in (2, 3, 1, 0):
        arrive_w(rep_of(1, 2, 0), piece)
        send_w(rep_of(1, 2, 0), piece, sibling)
    both_w(1, 2)
    project(1, 2)

    def head_norm(s, carry):
        rows = pl.ds(pl.multiple_of(s * SEQS, SEQS), SEQS)
        cosine = tables[0, rows, :]
        sine = tables[1, rows, :]
        for head in range(9):
            h, lanes = (0, head) if head < 5 else (1, head - 5)
            cols = pl.ds(lanes * HEAD_DIM, HEAD_DIM)
            values = acc[h, rows, cols]
            gain = q_gain[...] if head < 8 else k_gain[...]
            mean = jnp.sum(values * values, axis=1, keepdims=True) / HEAD_DIM
            values = values * lax.rsqrt(mean + norm_eps) * gain
            acc[h, rows, cols] = values * cosine + pltpu.roll(values, 64, 1) * sine
        cols = pl.ds(512, HEAD_DIM)
        acc[1, rows, cols] = acc[1, rows, cols] * scales[2]
        return carry

    lax.fori_loop(0, STEPS, head_norm, 0)

    for load in loads[8:]:
        load.wait()

    old_seq = lax.broadcasted_iota(jnp.int32, (8, 8 * CACHE), 0)
    old_col = lax.broadcasted_iota(jnp.int32, (8, 8 * CACHE), 1)
    old_slot = jnp.where(
        jnp.right_shift(old_col, 6) == old_seq, jnp.bitwise_and(old_col, CACHE - 1), CACHE
    ).astype(F32)
    new_row = lax.broadcasted_iota(jnp.int32, (32, 32), 0)
    new_col = lax.broadcasted_iota(jnp.int32, (32, 32), 1)
    new_live = (jnp.bitwise_and(new_row, 7) == jnp.bitwise_and(new_col, 7)) & (
        jnp.right_shift(new_col, 3) <= jnp.right_shift(new_row, 3)
    )
    new_bias = jnp.where(new_live, 0.0, -1e30)
    scaling = HEAD_DIM ** (-0.5)
    nt = (((1,), (1,)), ((), ()))

    def attend_eight(g):
        seqs = pl.ds(pl.multiple_of(g * 8, 8), 8)

        def pick(h, lanes):
            return [
                acc[h, pl.ds(pl.multiple_of(s * SEQS + g * 8, 8), 8), pl.ds(lanes * HEAD_DIM, HEAD_DIM)]
                for s in range(STEPS)
            ]

        rows = []
        for head in range(8):
            rows += pick(0, head) if head < 5 else pick(1, head - 5)
        queries = jnp.concatenate(rows, axis=0).astype(BF)
        fresh_keys = jnp.concatenate(pick(1, 3), axis=0).astype(BF)
        fresh_values = jnp.concatenate(pick(1, 4), axis=0).astype(BF)
        old_keys = keys_in[seqs].reshape(8 * CACHE, HEAD_DIM)
        old_values = values_in[seqs].reshape(8 * CACHE, HEAD_DIM)
        old_bias = jnp.where(old_slot < seq_len[seqs, :], 0.0, -1e30)
        old = lax.dot_general(queries, old_keys, nt, preferred_element_type=F32)
        new = lax.dot_general(queries, fresh_keys, nt, preferred_element_type=F32)
        old = (old.reshape(32, 8, 8 * CACHE) * scaling + old_bias[None]).reshape(256, 8 * CACHE)
        new = (new.reshape(8, 32, 32) * scaling + new_bias[None]).reshape(256, 32)
        top = jnp.maximum(
            jnp.max(old, axis=1, keepdims=True), jnp.max(new, axis=1, keepdims=True)
        )
        old = jnp.exp(old - top)
        new = jnp.exp(new - top)
        total = jnp.sum(old, axis=1, keepdims=True) + jnp.sum(new, axis=1, keepdims=True)
        result = dot(old.astype(BF), old_values) + dot(new.astype(BF), fresh_values)
        return result / total

    def attend(g, carry):
        low = attend_eight(g * 2)
        high = attend_eight(g * 2 + 1)
        for head in range(8):
            for s in range(STEPS):
                start = head * 32 + s * 8
                pair = jnp.concatenate([low[start : start + 8], high[start : start + 8]], axis=0)
                attb[
                    pl.ds(pl.multiple_of(s * SEQS + g * 16, 16), 16),
                    pl.ds(head * HEAD_DIM, HEAD_DIM),
                ] = pair.astype(BF)
        return carry

    lax.fori_loop(0, SEQS // 16, attend, 0)

    x_up = ((line_x + 1) % 4) * 2 + line_y
    x_down = ((line_x + 3) % 4) * 2 + line_y
    y_mate = line_x * 2 + 1 - line_y
    low, high = (0, LOW), (LOW, ROWS - LOW)

    def push(index, block, rows, spot, target):
        return pltpu.make_async_remote_copy(
            src_ref=rows_in.at[block, pl.ds(*rows)],
            dst_ref=rs_recv.at[spot[0], pl.ds(spot[1], rows[1])],
            send_sem=rs_s.at[index],
            recv_sem=rs_r.at[index],
            device_id=at_tp(target),
            device_id_type=MESH,
        )

    def line(index, base, spot, rows):
        half = rows[1] // 2
        first, second = (rows[0], half), (rows[0] + half, half)
        return [
            push(index, base + 2, first, (spot, first[0]), x_up),
            push(index + 1, base + 2, second, (spot, second[0]), x_down),
            push(index + 2, base + 1, second, (spot + 1, second[0]), x_up),
            push(index + 3, base + 1, first, (spot + 1, first[0]), x_up),
            push(index + 4, base + 3, first, (spot + 2, first[0]), x_down),
            push(index + 5, base + 3, second, (spot + 2, second[0]), x_down),
        ]

    to_mate = [push(k, k, low, (4 + k, 0), y_mate) for k in range(4)]
    other_high = line(4, 0, 4, high)
    this_high = line(10, 4, 1, high)
    this_low = line(16, 4, 1, low)
    last = push(22, 0, high, (7, LOW), y_mate)

    def begin(copies, k):
        for index in {1: (2,), 2: (0, 1), 3: (4,), 0: ()}[k]:
            copies[index].start()

    def carry_on(copies, base, spot, rows):
        half = rows[1] // 2
        for index, block, first in ((0, 1, rows[0]), (1, 3, rows[0] + half)):
            copies[index].wait_recv()
            where = pl.ds(first, half)
            rows_in[base + block, where, :] = (
                rows_in[base + block, where, :].astype(F32) + rs_recv[spot, where, :].astype(F32)
            ).astype(BF)
            copies[3 if index == 0 else 5].start()

    def partial(k, row, rows):
        owner = ((line_x + k) % 4) * 2 + row
        weights = obuf[pl.ds(owner * 2, 2)].reshape(HALF, Q_LOCAL)
        return lax.dot_general(attb[rows, :], weights, nt, preferred_element_type=F32)

    low_rows = slice(0, LOW)
    high_rows = slice(LOW, ROWS)

    def begin_at(copies, k):
        if isinstance(k, int):
            begin(copies, k)
            return
        for known in (1, 2, 3):
            pl.when(k == known)(lambda known=known: begin(copies, known))

    def emit_other(k):
        rows_in[k, low_rows, :] = partial(k, 1 - line_y, low_rows).astype(BF)
        push(k, k, low, (4 + k, 0), y_mate).start()
        rows_in[k, high_rows, :] = partial(k, 1 - line_y, high_rows).astype(BF)
        begin_at(other_high, k)

    def emit_this(k):
        rows_in[4 + k, high_rows, :] = partial(k, line_y, high_rows).astype(BF)
        begin_at(this_high, k)
        rows_in[4 + k, low_rows, :] = partial(k, line_y, low_rows).astype(BF)

    def pair_at(z_of):
        k = (z_of // 2 + 4 - line_x) % 4
        first = 1 + (k + 1) % 2
        return first, (first + 2) % 4

    near = pair_at(zz)
    across = pair_at((zz + 2) % 4)

    def from_mate():
        for k in (2, 1, 3, 0):
            to_mate[k].wait_recv()
            rows_in[4 + k, low_rows, :] = (
                rows_in[4 + k, low_rows, :].astype(F32) + rs_recv[4 + k, low_rows, :].astype(F32)
            ).astype(BF)
            begin(this_low, k)
        carry_on(this_low, 4, 1, low)

    other_first = (zz + 1) % 2 == 1 - line_y

    both_o(0, 0)
    both_o(1, 0)

    @pl.when(other_first)
    def _():
        for k in near:
            emit_this(k)

    @pl.when(jnp.logical_not(other_first))
    def _():
        for k in near:
            emit_other(k)

    beside_o(1)
    for dy in range(2):
        for dz in (1, 3):
            both_o(dy, dz)

    @pl.when(other_first)
    def _():
        for k in (2, 1, 3, 0):
            emit_other(k)
        carry_on(other_high, 0, 4, high)

    @pl.when(jnp.logical_not(other_first))
    def _():
        for k in (2, 1, 3, 0):
            emit_this(k)
        carry_on(this_high, 4, 1, high)

    across_o(0)
    across_o(1)
    for dy in range(2):
        both_o(dy, 2)

    @pl.when(other_first)
    def _():
        for k in across:
            emit_this(k)
        carry_on(this_high, 4, 1, high)

    @pl.when(jnp.logical_not(other_first))
    def _():
        for k in across:
            emit_other(k)
        carry_on(other_high, 0, 4, high)

    def sum_high():
        for index in range(2, 6):
            other_high[index].wait_recv()

        def add_up(i, carry):
            rows = pl.ds(pl.multiple_of(LOW + i * 32, 32), 32)
            total = rows_in[0, rows, :].astype(F32)
            for spot in (5, 6):
                total = total + rs_recv[spot, rows, :].astype(F32)
            rows_in[0, rows, :] = total.astype(BF)
            return carry

        lax.fori_loop(0, high[1] // 32, add_up, 0)
        last.start()

    @pl.when(other_first)
    def _():
        sum_high()
        from_mate()

    @pl.when(jnp.logical_not(other_first))
    def _():
        from_mate()
        sum_high()

    for copies in (this_low, this_high):
        for index in range(2, 6):
            copies[index].wait_recv()

    def finish_low(i, carry):
        rows = pl.ds(pl.multiple_of(i * 32, 32), 32)
        total = rows_in[4, rows, :].astype(F32)
        for spot in (2, 3):
            total = total + rs_recv[spot, rows, :].astype(F32)
        mixed[rows, :] = (resid[rows, :].astype(F32) + total * scales[3]).astype(BF)
        return carry

    lax.fori_loop(0, LOW // 32, finish_low, 0)
    last.wait_recv()

    def finish_high(i, carry):
        rows = pl.ds(pl.multiple_of(LOW + i * 32, 32), 32)
        total = rows_in[4, rows, :].astype(F32)
        for spot in (2, 3, 7):
            total = total + rs_recv[spot, rows, :].astype(F32)
        mixed[rows, :] = (resid[rows, :].astype(F32) + total * scales[3]).astype(BF)
        return carry

    lax.fori_loop(0, high[1] // 32, finish_high, 0)

    for copy in to_mate + other_high + this_high + this_low + [last]:
        copy.wait_send()
    for copy in a2a + sent_w + sent_o:
        copy.wait_send()
    fold(am_c, 4, [11])
    for m in range(4):
        new_history[m : m + 1, :] = jnp.where(
            slot == cycle[m],
            amax_out[5, m : m + 1, 0:1] * roots[m],
            history[m : m + 1, :],
        )


def shards(
    hidden_in,
    ln_gain,
    q_gain,
    k_gain,
    w_query,
    w_key,
    w_value,
    w_out,
    cache_keys,
    cache_values,
    cache_lengths,
    amax_history,
    cycle_pos,
):
    half_dim = HEAD_DIM // 2
    inverse = rope_base ** (-(2.0 * np.arange(half_dim)) / HEAD_DIM)
    freq = jnp.asarray(np.concatenate([inverse, inverse])[None, :], F32)
    vmem = pl.BlockSpec(memory_space=pltpu.VMEM)
    smem = pl.BlockSpec(memory_space=pltpu.SMEM)
    hbm = pl.BlockSpec(memory_space=pl.ANY)
    dma = pltpu.SemaphoreType.DMA
    mixed, new_history = pl.pallas_call(
        kernel,
        out_shape=(
            jax.ShapeDtypeStruct((ROWS, HALF), BF),
            jax.ShapeDtypeStruct((4, HIST), F32),
        ),
        in_specs=[hbm, vmem, vmem, vmem, vmem, vmem, vmem, vmem, hbm, hbm, vmem, vmem, smem]
        + [vmem],
        out_specs=(vmem, vmem),
        scratch_shapes=[
            pltpu.VMEM((SPOTS, ROWS, HALF), BF),
            pltpu.VMEM((SEQS, CACHE, HEAD_DIM), BF),
            pltpu.VMEM((SEQS, CACHE, HEAD_DIM), BF),
            pltpu.VMEM((TPS, PACKED, HALF), BF),
            pltpu.VMEM((REPS, TPS, PACKED, HALF), BF),
            pltpu.VMEM((REPS, OUT_SHARD, Q_LOCAL), BF),
            pltpu.VMEM((2, HALF, 768), BF),
            pltpu.VMEM((SPOTS, 2, ROWS, 768), BF),
            pltpu.VMEM((2, ROWS, HEAD_DIM), F32),
            pltpu.VMEM((SEQS, 1), F32),
            pltpu.VMEM((2, ROWS, HALF), F32),
            pltpu.VMEM((ROWS, Q_LOCAL), BF),
            pltpu.VMEM((8, ROWS, HALF), BF),
            pltpu.VMEM((ROWS, HALF), BF),
            pltpu.VMEM((6, 8, 128), F32),
            pltpu.VMEM((12, 8, 128), F32),
            dma((12,)),
            dma((7,)),
            dma((7,)),
            dma((60,)),
            dma((REPS, 4)),
            dma((30,)),
            dma((REPS, 2)),
            dma((23,)),
            dma((23,)),
            dma((12,)),
            dma((12,)),
        ],
        compiler_params=pltpu.CompilerParams(
            collective_id=0, has_side_effects=True, vmem_limit_bytes=62 * 2**20
        ),
        cost_estimate=pl.CostEstimate(
            flops=13 * 10**9, bytes_accessed=13 * 10**6, transcendentals=10**6
        ),
    )(
        hidden_in.reshape(ROWS, D),
        ln_gain.reshape(1, D),
        q_gain.reshape(1, HEAD_DIM),
        k_gain.reshape(1, HEAD_DIM),
        w_query,
        w_key,
        w_value,
        w_out.T,
        cache_keys,
        cache_values,
        cache_lengths.reshape(1, SEQS),
        amax_history,
        cycle_pos,
        freq,
    )
    return mixed.reshape(STEPS, SEQS, HALF), new_history


def solution(mesh):
    placed = (
        P(None, "rep", None),
        P(),
        P(),
        P(),
        P(("rep", "tp"), None),
        P(("rep", "tp"), None),
        P(("rep", "tp"), None),
        P("tp", "rep"),
        P("rep", None, "tp"),
        P("rep", None, "tp"),
        P("rep"),
        P(),
        P(),
    )
    return jax.shard_map(
        shards, mesh=mesh, in_specs=placed, out_specs=(P(None, "rep", "tp"), P()), check_vma=False
    )
```

```python
import jax
import jax.numpy as jnp
import numpy as np
from jax import lax
from jax.experimental import pallas as pl
from jax.experimental.pallas import tpu as pltpu
from jax.sharding import PartitionSpec as P

D = 5120
HEADS = 64
KV_HEADS = 8
HEAD_DIM = 128
STEPS = 4
HIST = 16
WINDOW = 8
Q_WIDTH = 8192
CACHE = 64
SEQS = 128
ROWS = STEPS * SEQS
REPS = 16
TPS = 8
SPOTS = 8
SHARD = 40
Q_LOCAL = 1024
HALF = 640
PACKED = 80
OUT_SHARD = 320
LOW = 224
PLANES = ((0, 0), (0, 1), (1, 0), (3, 0), (1, 1), (3, 1), (2, 0), (2, 1))
W_PIECES = ((5, 3), (2, 3), (0, 1), (1, 1))
O_PIECES = ((0, 160), (160, 160))

fp8_top = 448.0
rope_base = 1000000.0
norm_eps = 1e-06

BF = jnp.bfloat16
F32 = jnp.float32
MESH = pl.DeviceIdType.MESH


def dot(a, b):
    return jnp.dot(a, b, preferred_element_type=F32)


def quantize(weight, factor):
    return jnp.clip(weight.astype(F32) / factor, -fp8_top, fp8_top)


def kernel(
    hidden,
    ln_gain,
    q_gain,
    k_gain,
    w_query,
    w_key,
    w_value,
    w_out,
    cache_keys,
    cache_values,
    lengths,
    history,
    cycle,
    freq,
    mixed,
    new_history,
    rows_in,
    keys_in,
    values_in,
    stage,
    wbuf,
    obuf,
    spread,
    xs,
    tables,
    seq_len,
    acc,
    attb,
    rs_recv,
    resid,
    amax_out,
    amax_in,
    local_sem,
    a2a_s,
    a2a_r,
    w_s,
    w_r,
    o_s,
    o_r,
    rs_s,
    rs_r,
    am_s,
    am_r,
):
    rep = lax.axis_index("rep")
    tp = lax.axis_index("tp")
    yh = rep // 8
    zz = (rep // 2) % 4
    core = rep % 2
    spot = rep // 2

    def rep_of(dy, dz, flip):
        return ((yh + dy) % 2) * 8 + ((zz + dz) % 4) * 2 + (core + flip) % 2

    def spot_of(dy, dz):
        return ((yh + dy) % 2) * 4 + (zz + dz) % 4

    def at_rep(index):
        return {"rep": index, "tp": tp}

    def at_tp(index):
        return {"rep": rep, "tp": index}

    y_far = rep_of(1, 0, 0)
    z_up = rep_of(0, 1, 0)
    z_down = rep_of(0, 3, 0)
    sibling = rep_of(0, 0, 1)
    line_x = tp // 2
    line_y = tp % 2
    peers = [((line_x + kx) % 4) * 2 + (line_y + ky) % 2 for kx, ky in PLANES[1:]]

    loads = []
    for i in range(SPOTS):
        loads.append(
            pltpu.make_async_copy(hidden.at[:, pl.ds(i * HALF, HALF)], rows_in.at[i], local_sem.at[i])
        )
    loads.append(pltpu.make_async_copy(cache_keys, keys_in, local_sem.at[8]))
    loads.append(pltpu.make_async_copy(cache_values, values_in, local_sem.at[9]))
    loads.append(
        pltpu.make_async_copy(
            hidden.at[:, pl.ds(pl.multiple_of(tp * HALF, 128), HALF)], resid, local_sem.at[10]
        )
    )
    for load in loads:
        load.start()

    barrier = pltpu.get_barrier_semaphore()
    for peer in peers:
        pl.semaphore_signal(barrier, inc=1, device_id=at_tp(peer), device_id_type=MESH)
    for other in (y_far, z_up, z_down, sibling):
        pl.semaphore_signal(barrier, inc=1, device_id=at_rep(other), device_id_type=MESH)

    slot = lax.broadcasted_iota(jnp.int32, (1, HIST), 1)
    fans = (D, D, D, Q_WIDTH)
    roots = [float(np.sqrt(np.float32(fan))) for fan in fans]
    scales = []
    for m in range(4):
        behind = jnp.bitwise_and(cycle[m] + (2 * HIST - 1) - slot, HIST - 1)
        limit = jnp.max(
            jnp.where(behind < WINDOW, history[m : m + 1, :], 0.0), axis=1, keepdims=True
        )
        scales.append(limit / (fp8_top * roots[m]))

    def pack(j, tops):
        query = w_query[:, pl.ds(pl.multiple_of(j * Q_LOCAL, 128), Q_LOCAL)]
        key = w_key[:, pl.ds(pl.multiple_of(j * 128, 128), 128)]
        value = w_value[:, pl.ds(pl.multiple_of(j * 128, 128), 128)]
        q0 = quantize(query, scales[0])
        k0 = quantize(key, scales[1])
        v0 = quantize(value, scales[2])
        first = q0[:, :HALF]
        second = jnp.concatenate([q0[:, HALF:], k0, v0], axis=1)
        stage[j, 0:32, :] = first[0:32].astype(BF)
        stage[j, 32:48, :] = jnp.concatenate([first[32:40], second[32:40]], axis=0).astype(BF)
        stage[j, 48:80, :] = second[0:32].astype(BF)

        def top(values, old):
            found = jnp.max(jnp.abs(values.astype(F32)), axis=0, keepdims=True)
            for i in range(values.shape[1] // 128):
                old = jnp.maximum(old, found[:, i * 128 : (i + 1) * 128])
            return old

        return top(query, tops[0]), top(key, tops[1]), top(value, tops[2])

    none = jnp.zeros((1, 128), F32)
    tops = lax.fori_loop(0, TPS, pack, (none, none, none))

    pl.semaphore_wait(barrier, 11)

    a2a = []
    for s, peer in enumerate(peers):
        a2a.append(
            pltpu.make_async_remote_copy(
                src_ref=stage.at[peer],
                dst_ref=wbuf.at[rep, s + 1],
                send_sem=a2a_s.at[s],
                recv_sem=a2a_r.at[s],
                device_id=at_tp(peer),
                device_id_type=MESH,
            )
        )
    for copy in a2a:
        copy.start()
    own_plane = pltpu.make_async_copy(stage.at[tp], wbuf.at[rep, 0], local_sem.at[11])
    own_plane.start()

    def relay(buf, pieces, send_sem, recv_sem):
        sent = []

        def send(block, piece, *targets):
            view = buf.at[block, pl.ds(*pieces[piece])]
            for target in targets:
                copy = pltpu.make_async_remote_copy(
                    src_ref=view,
                    dst_ref=view,
                    send_sem=send_sem.at[len(sent)],
                    recv_sem=recv_sem.at[block, piece],
                    device_id=at_rep(target),
                    device_id_type=MESH,
                )
                copy.start()
                sent.append(copy)

        def arrive(block, *which):
            for piece in which or range(len(pieces)):
                view = buf.at[block, pl.ds(*pieces[piece])]
                pltpu.make_async_remote_copy(
                    src_ref=view,
                    dst_ref=view,
                    send_sem=send_sem.at[0],
                    recv_sem=recv_sem.at[block, piece],
                    device_id=at_rep(sibling),
                    device_id_type=MESH,
                ).wait_recv()

        return send, arrive, sent

    send_w, arrive_w, sent_w = relay(wbuf, W_PIECES, w_s, w_r)
    send_o, arrive_o, sent_o = relay(obuf, O_PIECES, o_s, o_r)

    def both_w(dy, dz):
        arrive_w(rep_of(dy, dz, 1))

    def both_o(dy, dz):
        arrive_o(rep_of(dy, dz, 1))

    def far_o():
        for piece in range(2):
            arrive_o(y_far, piece)
            send_o(y_far, piece, z_up, z_down, sibling)

    def beside_o(dy):
        for piece in range(2):
            for dz, target, keep in ((1, z_down, 0), (3, z_up, 1)):
                block = rep_of(dy, dz, 0)
                arrive_o(block, piece)
                if piece == keep:
                    send_o(block, piece, target)
                send_o(block, piece, sibling)

    def across_o(dy):
        for piece in range(2):
            arrive_o(rep_of(dy, 2, 0), piece)
            send_o(rep_of(dy, 2, 0), piece, sibling)

    own_plane.wait()
    send_w(rep, 2, z_up, z_down, y_far, sibling)

    def pack_out(i, old):
        rows = pl.ds(pl.multiple_of(i * 32, 32), 32)
        shard = w_out[rows, :]
        obuf[rep, rows, :] = quantize(shard, scales[3]).astype(BF)
        found = jnp.max(jnp.abs(shard.astype(F32)), axis=0, keepdims=True)
        return jnp.maximum(old, jnp.max(found, axis=1, keepdims=True))

    top_out = lax.fori_loop(0, OUT_SHARD // 32, pack_out, jnp.zeros((1, 1), F32))

    a2a[0].wait_recv()
    send_w(rep, 3, z_up, z_down, y_far, sibling)
    for piece in range(2):
        send_o(rep, piece, z_up, z_down, sibling)

    tile_row = lax.broadcasted_iota(jnp.int32, (8, 128), 0)
    found = [jnp.max(top, axis=1, keepdims=True) for top in tops] + [top_out]
    tile = jnp.zeros((8, 128), F32)
    for m in range(4):
        tile = jnp.where(tile_row == m, found[m], tile)
    amax_out[0] = tile

    def send_amax(stage_index, slot_index, where):
        return pltpu.make_async_remote_copy(
            src_ref=amax_out.at[stage_index],
            dst_ref=amax_in.at[slot_index],
            send_sem=am_s.at[slot_index],
            recv_sem=am_r.at[slot_index],
            device_id=where,
            device_id_type=MESH,
        )

    am_tp = [send_amax(0, s, at_tp(peer)) for s, peer in enumerate(peers)]
    am_y = [send_amax(1, 7, at_rep(y_far))]
    am_z = [send_amax(2, 8, at_rep(z_up)), send_amax(2, 9, at_rep(z_down))]
    am_w = [send_amax(3, 10, at_rep(z_up))]
    am_c = [send_amax(4, 11, at_rep(sibling))]

    def fold(copies, index, slots):
        for copy in copies:
            copy.wait()
        total = amax_out[index]
        for where in slots:
            total = jnp.maximum(total, amax_in[where])
        amax_out[index + 1] = total

    for copy in am_tp:
        copy.start()

    for load in loads[:8]:
        load.wait()

    def norm(i, carry):
        rows = pl.ds(pl.multiple_of(i * 32, 32), 32)
        parts = [rows_in[j, rows, :].astype(F32) for j in range(SPOTS)]
        square = parts[0] * parts[0]
        for part in parts[1:]:
            square = square + part * part
        mean = jnp.sum(square, axis=1, keepdims=True) / D
        factor = lax.rsqrt(mean + norm_eps)
        for j in range(SPOTS):
            gain = ln_gain[0:1, j * HALF : (j + 1) * HALF]
            rows_in[j, rows, :] = (parts[j] * factor * gain).astype(BF)
        return carry

    for copy in a2a[1:4]:
        copy.wait_recv()
    send_w(rep, 1, y_far, z_up, z_down, sibling)
    def beside_first(piece):
        for dz, target, keep in ((1, z_down, 2), (3, z_up, 3)):
            block = rep_of(0, dz, 0)
            arrive_w(block, piece)
            if piece == keep:
                send_w(block, piece, target)
            send_w(block, piece, y_far, sibling)

    beside_first(2)
    for copy in a2a[4:]:
        copy.wait_recv()
    send_w(rep, 0, y_far, z_up, z_down, sibling)
    beside_first(3)
    for piece in range(2):
        send_o(rep, piece, y_far)
    lax.fori_loop(0, ROWS // 32, norm, 0)

    diagonal = lax.broadcasted_iota(jnp.int32, (SEQS, SEQS), 0) == lax.broadcasted_iota(
        jnp.int32, (SEQS, SEQS), 1
    )
    seq_len[...] = jnp.sum(
        jnp.where(diagonal, lengths[...].astype(F32), 0.0), axis=1, keepdims=True
    )
    lane = lax.broadcasted_iota(jnp.int32, (SEQS, HEAD_DIM), 1)

    def turn(s, carry):
        rows = pl.ds(pl.multiple_of(s * SEQS, SEQS), SEQS)
        angles = (seq_len[...] + lax.convert_element_type(s, F32)) * freq[...]
        tables[0, rows, :] = jnp.cos(angles)
        sine = jnp.sin(angles)
        tables[1, rows, :] = jnp.where(lane < 64, -sine, sine)
        return carry

    column = lax.broadcasted_iota(jnp.int32, (1, 768), 1)
    block_of = jnp.right_shift(column * 1366, 16)
    inside = column - block_of * 48
    plane = jnp.bitwise_and(block_of, 7)
    off_x = jnp.zeros_like(plane)
    off_y = jnp.zeros_like(plane)
    for n, (kx, ky) in enumerate(PLANES):
        off_x = jnp.where(plane == n, kx, off_x)
        off_y = jnp.where(plane == n, ky, off_y)
    block_of = (
        block_of
        - plane
        + jnp.bitwise_and(line_x + 4 - off_x, 3) * 2
        + jnp.bitwise_and(line_y + off_y, 1)
    )
    wanted = (
        jnp.where(inside < 40, block_of * SHARD + inside, -1),
        jnp.where(
            inside < 8,
            -1,
            block_of * SHARD + jnp.where(inside < 16, inside + 24, inside - 16),
        ),
    )
    for h in range(2):
        for part in range(5):
            row = lax.broadcasted_iota(jnp.int32, (128, 768), 0) + part * 128
            spread[h, part * 128 : (part + 1) * 128, :] = jnp.where(
                row == wanted[h], 1.0, 0.0
            ).astype(BF)

    lax.fori_loop(0, STEPS, turn, 0)

    acc[...] = jnp.zeros_like(acc)

    def select(dy, dz):
        place = spot_of(dy, dz)

        def tiles(i, carry):
            rows = pl.ds(pl.multiple_of(i * 256, 256), 256)
            for h in range(2):
                xs[place, h, rows, :] = dot(rows_in[place, rows, :], spread[h]).astype(BF)
            return carry

        lax.fori_loop(0, 2, tiles, 0)

    def project(dy, dz):
        place = spot_of(dy, dz)

        def tiles(i, carry):
            rows = pl.ds(pl.multiple_of(i * 256, 256), 256)
            for h in range(2):
                block = wbuf[pl.ds(place * 2, 2), :, h * 32 : h * 32 + 48, :].reshape(768, HALF)
                acc[h, rows, :] = acc[h, rows, :] + dot(xs[place, h, rows, :], block)
            return carry

        lax.fori_loop(0, 2, tiles, 0)

    select(0, 0)
    select(1, 0)
    select(0, 1)
    for piece in (1, 0):
        arrive_w(y_far, piece)
        send_w(y_far, piece, z_up, z_down, sibling)
    both_w(0, 0)
    project(0, 0)
    select(0, 3)
    fold(am_tp, 0, range(7))
    am_y[0].start()
    for piece in (1, 0):
        for dz, target, keep in ((1, z_down, 0), (3, z_up, 1)):
            block = rep_of(0, dz, 0)
            arrive_w(block, piece)
            if piece == keep:
                send_w(block, piece, target)
            send_w(block, piece, sibling)
    for piece in (2, 3):
        arrive_w(y_far, piece)
        send_w(y_far, piece, sibling)
    both_w(0, 1)
    project(0, 1)
    select(1, 1)
    for piece in (2, 3):
        arrive_w(rep_of(0, 2, 0), piece)
        send_w(rep_of(0, 2, 0), piece, y_far, sibling)
    both_w(0, 3)
    project(0, 3)
    both_w(1, 0)
    project(1, 0)
    select(1, 3)
    fold(am_y, 1, [7])
    for copy in am_z:
        copy.start()
    for piece in (2, 3):
        for dz in (1, 3):
            arrive_w(rep_of(1, dz, 0), piece)
            send_w(rep_of(1, dz, 0), piece, sibling)
    select(0, 2)
    for piece in (1, 0):
        for dz, target, keep in ((1, z_down, 0), (3, z_up, 1)):
            block = rep_of(1, dz, 0)
            arrive_w(block, piece)
            if piece == keep:
                send_w(block, piece, target)
            send_w(block, piece, sibling)
    select(1, 2)
    both_w(1, 1)
    project(1, 1)
    fold(am_z, 2, [8, 9])
    am_w[0].start()
    for piece in (1, 0):
        arrive_w(rep_of(0, 2, 0), piece)
        send_w(rep_of(0, 2, 0), piece, sibling)
    both_w(1, 3)
    project(1, 3)
    both_w(0, 2)
    project(0, 2)
    fold(am_w, 3, [10])
    am_c[0].start()
    for piece in (2, 3, 1, 0):
        arrive_w(rep_of(1, 2, 0), piece)
        send_w(rep_of(1, 2, 0), piece, sibling)
    far_o()
    beside_o(0)
    both_w(1, 2)
    project(1, 2)

    def head_norm(s, carry):
        rows = pl.ds(pl.multiple_of(s * SEQS, SEQS), SEQS)
        cosine = tables[0, rows, :]
        sine = tables[1, rows, :]
        for head in range(9):
            h, lanes = (0, head) if head < 5 else (1, head - 5)
            cols = pl.ds(lanes * HEAD_DIM, HEAD_DIM)
            values = acc[h, rows, cols]
            gain = q_gain[...] if head < 8 else k_gain[...]
            mean = jnp.sum(values * values, axis=1, keepdims=True) / HEAD_DIM
            values = values * lax.rsqrt(mean + norm_eps) * gain
            acc[h, rows, cols] = values * cosine + pltpu.roll(values, 64, 1) * sine
        cols = pl.ds(512, HEAD_DIM)
        acc[1, rows, cols] = acc[1, rows, cols] * scales[2]
        return carry

    lax.fori_loop(0, STEPS, head_norm, 0)

    for load in loads[8:]:
        load.wait()

    old_seq = lax.broadcasted_iota(jnp.int32, (8, 8 * CACHE), 0)
    old_col = lax.broadcasted_iota(jnp.int32, (8, 8 * CACHE), 1)
    old_slot = jnp.where(
        jnp.right_shift(old_col, 6) == old_seq, jnp.bitwise_and(old_col, CACHE - 1), CACHE
    ).astype(F32)
    new_row = lax.broadcasted_iota(jnp.int32, (32, 32), 0)
    new_col = lax.broadcasted_iota(jnp.int32, (32, 32), 1)
    new_live = (jnp.bitwise_and(new_row, 7) == jnp.bitwise_and(new_col, 7)) & (
        jnp.right_shift(new_col, 3) <= jnp.right_shift(new_row, 3)
    )
    new_bias = jnp.where(new_live, 0.0, -1e30)
    scaling = HEAD_DIM ** (-0.5)
    nt = (((1,), (1,)), ((), ()))

    def attend_eight(g):
        seqs = pl.ds(pl.multiple_of(g * 8, 8), 8)

        def pick(h, lanes):
            return [
                acc[h, pl.ds(pl.multiple_of(s * SEQS + g * 8, 8), 8), pl.ds(lanes * HEAD_DIM, HEAD_DIM)]
                for s in range(STEPS)
            ]

        rows = []
        for head in range(8):
            rows += pick(0, head) if head < 5 else pick(1, head - 5)
        queries = jnp.concatenate(rows, axis=0).astype(BF)
        fresh_keys = jnp.concatenate(pick(1, 3), axis=0).astype(BF)
        fresh_values = jnp.concatenate(pick(1, 4), axis=0).astype(BF)
        old_keys = keys_in[seqs].reshape(8 * CACHE, HEAD_DIM)
        old_values = values_in[seqs].reshape(8 * CACHE, HEAD_DIM)
        old_bias = jnp.where(old_slot < seq_len[seqs, :], 0.0, -1e30)
        old = lax.dot_general(queries, old_keys, nt, preferred_element_type=F32)
        new = lax.dot_general(queries, fresh_keys, nt, preferred_element_type=F32)
        old = (old.reshape(32, 8, 8 * CACHE) * scaling + old_bias[None]).reshape(256, 8 * CACHE)
        new = (new.reshape(8, 32, 32) * scaling + new_bias[None]).reshape(256, 32)
        top = jnp.maximum(
            jnp.max(old, axis=1, keepdims=True), jnp.max(new, axis=1, keepdims=True)
        )
        old = jnp.exp(old - top)
        new = jnp.exp(new - top)
        total = jnp.sum(old, axis=1, keepdims=True) + jnp.sum(new, axis=1, keepdims=True)
        result = dot(old.astype(BF), old_values) + dot(new.astype(BF), fresh_values)
        return result / total

    def attend(g, carry):
        low = attend_eight(g * 2)
        high = attend_eight(g * 2 + 1)
        for head in range(8):
            for s in range(STEPS):
                start = head * 32 + s * 8
                pair = jnp.concatenate([low[start : start + 8], high[start : start + 8]], axis=0)
                attb[
                    pl.ds(pl.multiple_of(s * SEQS + g * 16, 16), 16),
                    pl.ds(head * HEAD_DIM, HEAD_DIM),
                ] = pair.astype(BF)
        return carry

    lax.fori_loop(0, SEQS // 16, attend, 0)

    x_up = ((line_x + 1) % 4) * 2 + line_y
    x_down = ((line_x + 3) % 4) * 2 + line_y
    y_mate = line_x * 2 + 1 - line_y
    low, high = (0, LOW), (LOW, ROWS - LOW)

    def push(index, block, rows, spot, target):
        return pltpu.make_async_remote_copy(
            src_ref=rows_in.at[block, pl.ds(*rows)],
            dst_ref=rs_recv.at[spot[0], pl.ds(spot[1], rows[1])],
            send_sem=rs_s.at[index],
            recv_sem=rs_r.at[index],
            device_id=at_tp(target),
            device_id_type=MESH,
        )

    def line(index, base, spot, rows):
        half = rows[1] // 2
        first, second = (rows[0], half), (rows[0] + half, half)
        return [
            push(index, base + 2, first, (spot, first[0]), x_up),
            push(index + 1, base + 2, second, (spot, second[0]), x_down),
            push(index + 2, base + 1, second, (spot + 1, second[0]), x_up),
            push(index + 3, base + 1, first, (spot + 1, first[0]), x_up),
            push(index + 4, base + 3, first, (spot + 2, first[0]), x_down),
            push(index + 5, base + 3, second, (spot + 2, second[0]), x_down),
        ]

    to_mate = [push(k, k, low, (4 + k, 0), y_mate) for k in range(4)]
    other_high = line(4, 0, 4, high)
    this_high = line(10, 4, 1, high)
    this_low = line(16, 4, 1, low)
    last = push(22, 0, high, (7, LOW), y_mate)

    def begin(copies, k):
        for index in {1: (2,), 2: (0, 1), 3: (4,), 0: ()}[k]:
            copies[index].start()

    def carry_on(copies, base, spot, rows):
        half = rows[1] // 2
        for index, block, first in ((0, 1, rows[0]), (1, 3, rows[0] + half)):
            copies[index].wait_recv()
            where = pl.ds(first, half)
            rows_in[base + block, where, :] = (
                rows_in[base + block, where, :].astype(F32) + rs_recv[spot, where, :].astype(F32)
            ).astype(BF)
            copies[3 if index == 0 else 5].start()

    def partial(k, row, rows):
        owner = ((line_x + k) % 4) * 2 + row
        weights = obuf[pl.ds(owner * 2, 2)].reshape(HALF, Q_LOCAL)
        return lax.dot_general(attb[rows, :], weights, nt, preferred_element_type=F32)

    low_rows = slice(0, LOW)
    high_rows = slice(LOW, ROWS)

    def begin_at(copies, k):
        if isinstance(k, int):
            begin(copies, k)
            return
        for known in (1, 2, 3):
            pl.when(k == known)(lambda known=known: begin(copies, known))

    def emit_other(k):
        rows_in[k, low_rows, :] = partial(k, 1 - line_y, low_rows).astype(BF)
        push(k, k, low, (4 + k, 0), y_mate).start()
        rows_in[k, high_rows, :] = partial(k, 1 - line_y, high_rows).astype(BF)
        begin_at(other_high, k)

    def emit_this(k):
        rows_in[4 + k, high_rows, :] = partial(k, line_y, high_rows).astype(BF)
        begin_at(this_high, k)
        rows_in[4 + k, low_rows, :] = partial(k, line_y, low_rows).astype(BF)

    def pair_at(z_of):
        k = (z_of // 2 + 4 - line_x) % 4
        first = 1 + (k + 1) % 2
        return first, (first + 2) % 4

    near = pair_at(zz)
    across = pair_at((zz + 2) % 4)

    def from_mate():
        for k in (2, 1, 3, 0):
            to_mate[k].wait_recv()
            rows_in[4 + k, low_rows, :] = (
                rows_in[4 + k, low_rows, :].astype(F32) + rs_recv[4 + k, low_rows, :].astype(F32)
            ).astype(BF)
            begin(this_low, k)
        carry_on(this_low, 4, 1, low)

    other_first = (zz + 1) % 2 == 1 - line_y

    both_o(0, 0)
    both_o(1, 0)

    @pl.when(other_first)
    def _():
        for k in near:
            emit_this(k)

    @pl.when(jnp.logical_not(other_first))
    def _():
        for k in near:
            emit_other(k)

    beside_o(1)
    for dy in range(2):
        for dz in (1, 3):
            both_o(dy, dz)

    @pl.when(other_first)
    def _():
        for k in (2, 1, 3, 0):
            emit_other(k)
        carry_on(other_high, 0, 4, high)

    @pl.when(jnp.logical_not(other_first))
    def _():
        for k in (2, 1, 3, 0):
            emit_this(k)
        carry_on(this_high, 4, 1, high)

    across_o(0)
    across_o(1)
    for dy in range(2):
        both_o(dy, 2)

    @pl.when(other_first)
    def _():
        for k in across:
            emit_this(k)
        carry_on(this_high, 4, 1, high)

    @pl.when(jnp.logical_not(other_first))
    def _():
        for k in across:
            emit_other(k)
        carry_on(other_high, 0, 4, high)

    def sum_high():
        for index in range(2, 6):
            other_high[index].wait_recv()

        def add_up(i, carry):
            rows = pl.ds(pl.multiple_of(LOW + i * 32, 32), 32)
            total = rows_in[0, rows, :].astype(F32)
            for spot in (5, 6):
                total = total + rs_recv[spot, rows, :].astype(F32)
            rows_in[0, rows, :] = total.astype(BF)
            return carry

        lax.fori_loop(0, high[1] // 32, add_up, 0)
        last.start()

    @pl.when(other_first)
    def _():
        sum_high()
        from_mate()

    @pl.when(jnp.logical_not(other_first))
    def _():
        from_mate()
        sum_high()

    for copies in (this_low, this_high):
        for index in range(2, 6):
            copies[index].wait_recv()

    def finish_low(i, carry):
        rows = pl.ds(pl.multiple_of(i * 32, 32), 32)
        total = rows_in[4, rows, :].astype(F32)
        for spot in (2, 3):
            total = total + rs_recv[spot, rows, :].astype(F32)
        mixed[rows, :] = (resid[rows, :].astype(F32) + total * scales[3]).astype(BF)
        return carry

    lax.fori_loop(0, LOW // 32, finish_low, 0)
    last.wait_recv()

    def finish_high(i, carry):
        rows = pl.ds(pl.multiple_of(LOW + i * 32, 32), 32)
        total = rows_in[4, rows, :].astype(F32)
        for spot in (2, 3, 7):
            total = total + rs_recv[spot, rows, :].astype(F32)
        mixed[rows, :] = (resid[rows, :].astype(F32) + total * scales[3]).astype(BF)
        return carry

    lax.fori_loop(0, high[1] // 32, finish_high, 0)

    for copy in to_mate + other_high + this_high + this_low + [last]:
        copy.wait_send()
    for copy in a2a + sent_w + sent_o:
        copy.wait_send()
    fold(am_c, 4, [11])
    for m in range(4):
        new_history[m : m + 1, :] = jnp.where(
            slot == cycle[m],
            amax_out[5, m : m + 1, 0:1] * roots[m],
            history[m : m + 1, :],
        )


def shards(
    hidden_in,
    ln_gain,
    q_gain,
    k_gain,
    w_query,
    w_key,
    w_value,
    w_out,
    cache_keys,
    cache_values,
    cache_lengths,
    amax_history,
    cycle_pos,
):
    half_dim = HEAD_DIM // 2
    inverse = rope_base ** (-(2.0 * np.arange(half_dim)) / HEAD_DIM)
    freq = jnp.asarray(np.concatenate([inverse, inverse])[None, :], F32)
    vmem = pl.BlockSpec(memory_space=pltpu.VMEM)
    smem = pl.BlockSpec(memory_space=pltpu.SMEM)
    hbm = pl.BlockSpec(memory_space=pl.ANY)
    dma = pltpu.SemaphoreType.DMA
    mixed, new_history = pl.pallas_call(
        kernel,
        out_shape=(
            jax.ShapeDtypeStruct((ROWS, HALF), BF),
            jax.ShapeDtypeStruct((4, HIST), F32),
        ),
        in_specs=[hbm, vmem, vmem, vmem, vmem, vmem, vmem, vmem, hbm, hbm, vmem, vmem, smem]
        + [vmem],
        out_specs=(vmem, vmem),
        scratch_shapes=[
            pltpu.VMEM((SPOTS, ROWS, HALF), BF),
            pltpu.VMEM((SEQS, CACHE, HEAD_DIM), BF),
            pltpu.VMEM((SEQS, CACHE, HEAD_DIM), BF),
            pltpu.VMEM((TPS, PACKED, HALF), BF),
            pltpu.VMEM((REPS, TPS, PACKED, HALF), BF),
            pltpu.VMEM((REPS, OUT_SHARD, Q_LOCAL), BF),
            pltpu.VMEM((2, HALF, 768), BF),
            pltpu.VMEM((SPOTS, 2, ROWS, 768), BF),
            pltpu.VMEM((2, ROWS, HEAD_DIM), F32),
            pltpu.VMEM((SEQS, 1), F32),
            pltpu.VMEM((2, ROWS, HALF), F32),
            pltpu.VMEM((ROWS, Q_LOCAL), BF),
            pltpu.VMEM((8, ROWS, HALF), BF),
            pltpu.VMEM((ROWS, HALF), BF),
            pltpu.VMEM((6, 8, 128), F32),
            pltpu.VMEM((12, 8, 128), F32),
            dma((12,)),
            dma((7,)),
            dma((7,)),
            dma((60,)),
            dma((REPS, 4)),
            dma((30,)),
            dma((REPS, 2)),
            dma((23,)),
            dma((23,)),
            dma((12,)),
            dma((12,)),
        ],
        compiler_params=pltpu.CompilerParams(
            collective_id=0, has_side_effects=True, vmem_limit_bytes=62 * 2**20
        ),
        cost_estimate=pl.CostEstimate(
            flops=13 * 10**9, bytes_accessed=13 * 10**6, transcendentals=10**6
        ),
    )(
        hidden_in.reshape(ROWS, D),
        ln_gain.reshape(1, D),
        q_gain.reshape(1, HEAD_DIM),
        k_gain.reshape(1, HEAD_DIM),
        w_query,
        w_key,
        w_value,
        w_out.T,
        cache_keys,
        cache_values,
        cache_lengths.reshape(1, SEQS),
        amax_history,
        cycle_pos,
        freq,
    )
    return mixed.reshape(STEPS, SEQS, HALF), new_history


def solution(mesh):
    placed = (
        P(None, "rep", None),
        P(),
        P(),
        P(),
        P(("rep", "tp"), None),
        P(("rep", "tp"), None),
        P(("rep", "tp"), None),
        P("tp", "rep"),
        P("rep", None, "tp"),
        P("rep", None, "tp"),
        P("rep"),
        P(),
        P(),
    )
    return jax.shard_map(
        shards, mesh=mesh, in_specs=placed, out_specs=(P(None, "rep", "tp"), P()), check_vma=False
    )
```
